32 devices in a mesh: cells: 8 (over z, y), fsdp: 4 (over x, core).
Axes of the slice: x: 2, y: 2, z: 4, core: 2. Of those that a mesh axis runs over, the one named last changes fastest.
Arguments:
- tokens: bfloat16 [32, 1024, 512], P(('cells', 'fsdp')), may hold values from -6 to 6
- cotangent: bfloat16 [32, 1024, 512], P(('cells', 'fsdp')), may hold values from -6 to 6
- lengths: int32 [32], P(('cells', 'fsdp')), may hold values from 69 to 1024, as said below
- generate: int32 [32, 1024], P(('cells', 'fsdp')), may hold values 0 or 1
- qkv_weight: bfloat16 [512, 1536], P('fsdp'), may hold values from -0.25 to 0.25
- out_weight: bfloat16 [512, 512], P('fsdp'), may hold values from -2 to 2
- ff_in_weight: bfloat16 [512, 512], P('fsdp'), may hold values from -0.25 to 0.25
- ff_out_weight: bfloat16 [512, 512], P('fsdp'), may hold values from -0.25 to 0.25
- biases: bfloat16 [7, 512], P(None, 'fsdp'), may hold values from -1.75 to 1.75
- gains: bfloat16 [2, 512], P(None, 'fsdp'), may hold values from 0.25 to 1.75
Outputs:
- mixed: bfloat16 [32, 1024, 512], P(('cells', 'fsdp'))
- tokens_grad: float32 [32, 1024, 512], P(('cells', 'fsdp'))
- qkv_grad: float32 [512, 1536], P('fsdp')
- out_grad: float32 [512, 512], P('fsdp')
- ff_in_grad: float32 [512, 512], P('fsdp')
- ff_out_grad: float32 [512, 512], P('fsdp')
- biases_grad: float32 [7, 512], P(None, 'fsdp')
- gains_grad: float32 [2, 512], P(None, 'fsdp')
The draws below stay inside these ranges and needn't reach their ends.
Inputs may be any that keep to these rules, and one draw needn't show every extreme that they name: `lengths`: some cell in every draw has exactly 1024 gene tokens.
All inputs are finite; a program needn't handle non-finite values. No bound on the sum of `generate` on one device may be relied on, other than what follows from the above.
Results may differ from the reference program's by a relative error of at most 0.015.
The reference program's roundings to bfloat16 on the way count: a program that leaves them out, or rounds other values in their place, can miss the bound.
Values may be sent and summed in bfloat16 or wider, within the bound.
A program may use at most 128 MiB of HBM per device.

```python
import jax
import jax.numpy as jnp
from jax import lax

D = 512
H = 8
FF = 512
LEN = 1024
QB = 512
CELLS = 32


def draw_lengths(key, part):
    key = jax.random.fold_in(key, 7)
    first_key, second_key = jax.random.split(key)
    drawn = jax.random.randint(first_key, (CELLS,), LEN // 15 + 1, LEN + 1, dtype=jnp.int32)
    longest = jax.random.randint(second_key, (), 0, CELLS, dtype=jnp.int32)
    return jnp.where(jnp.arange(CELLS, dtype=jnp.int32) == longest, LEN, drawn).astype(jnp.int32)


def with_ends(values, own_key, smallest, largest):
    longest = values.shape.index(max(values.shape))
    spots = []
    for shift in (0, 1):
        where = [jax.random.randint(jax.random.fold_in(own_key, axis), (), 0, length) for axis, length in enumerate(values.shape)]
        where[longest] = (where[longest] + shift) % values.shape[longest]
        spots.append(tuple(where))
    return values.at[spots[0]].set(smallest).at[spots[1]].set(largest)


def steps_of(rng, extent, cuts, least, largest):
    def one(dim, shards_of):
        steps = jax.random.uniform(jax.random.fold_in(jax.random.fold_in(rng, 6), dim), (shards_of,), jnp.float32, least / len(cuts), largest / len(cuts))
        return jnp.repeat(jnp.exp(steps), extent[dim] // shards_of).reshape((-1,) + (1,) * (len(extent) - dim - 1))

    level = one(*cuts[0])
    for cut in cuts[1:]:
        level = level * one(*cut)
    return level


def normal_values(key, extent, scale, bound, cuts=(), held_as=jnp.bfloat16):
    values = jax.random.normal(key, extent, jnp.float32) * scale
    if len(cuts) > 0:
        values = steps_of(key, extent, cuts, -0.22, 0.18) * values
    return jnp.clip(values, min=-bound, max=bound).astype(held_as)


def setup_inputs(seed: int = 0) -> dict:
    splits = jax.random.split(jax.random.key(seed), 11)
    return {
        "tokens": normal_values(splits[0], (CELLS, LEN, D), 1.0, 6.0, ((0, 32),)),
        "cotangent": normal_values(splits[1], (CELLS, LEN, D), 1.0, 6.0, ((0, 32),)),
        "lengths": draw_lengths(jax.random.fold_in(splits[10], 71), 0),
        "generate": with_ends((jax.random.randint(splits[3], (CELLS, LEN), 0, 3) < 1).astype(jnp.int32), jax.random.fold_in(splits[3], 1), 0, 1),
        "qkv_weight": normal_values(splits[4], (D, 3 * D), D ** -0.5, 0.25, ((0, 4),)),
        "out_weight": normal_values(splits[5], (D, D), (D // 64) ** -0.5, 2.0, ((0, 4),)),
        "ff_in_weight": normal_values(splits[6], (D, FF), D ** -0.5, 0.25, ((0, 4),)),
        "ff_out_weight": normal_values(splits[7], (FF, D), FF ** -0.5, 0.25, ((0, 4),)),
        "biases": normal_values(splits[8], (7, D), 0.3, 1.75, ((1, 4),)),
        "gains": jnp.clip(1.0 + 0.15 * jax.random.normal(splits[9], (2, D), jnp.float32), 0.25, 1.75).astype(jnp.bfloat16),
    }


@jax.custom_vjp
def low(v):
    return lax.optimization_barrier(v.astype(jnp.bfloat16)).astype(jnp.float32)

@jax.custom_vjp
def low_back(v):
    return v

def low_keep(v):
    return (low(v), None)

def low_pass(kept, grad):
    return (grad,)

def back_keep(v):
    return (v, None)

def back_low(kept, grad):
    return (low(grad),)
low.defvjp(low_keep, low_pass)
low_back.defvjp(back_keep, back_low)
norm_eps = 1e-05

def matmul(left, right):
    return jnp.dot(left, right, precision=lax.Precision.HIGHEST)

def layer_norm(value, gain, shift):
    centre = lax.optimization_barrier(jnp.mean(value, axis=-1, keepdims=True))
    centred = value - centre
    spread = lax.optimization_barrier(jnp.mean(centred * centred, axis=-1, keepdims=True))
    return centred * lax.rsqrt(spread + norm_eps) * gain + shift

def allowed_mask(first_row, row_count, length, generate):
    row_ids = first_row + jnp.arange(row_count, dtype=jnp.int32)
    col_ids = jnp.arange(generate.shape[0], dtype=jnp.int32)
    visible = (col_ids < length) & (generate == 0)
    return (row_ids[:, None] == col_ids[None, :]) | visible[None, :]

def attend(queries, keys, values, length, generate):
    row_count, model_width = queries.shape
    head_size = model_width // H
    blocks = row_count // QB
    key_heads = keys.reshape(row_count, H, head_size)
    value_heads = values.reshape(row_count, H, head_size)

    def one_block(inputs_block):
        query_block, first_row = inputs_block
        allowed = allowed_mask(first_row, QB, length, generate)
        query_heads = query_block.reshape(QB, H, head_size)
        scores = jnp.einsum('qhd,khd->hqk', query_heads, key_heads, precision=lax.Precision.HIGHEST)
        scores = low_back(scores * head_size ** (-0.5))
        scores = jnp.where(allowed[None], scores, -1000000000.0)
        probs = low(jax.nn.softmax(scores, axis=-1))
        mixture = jnp.einsum('hqk,khd->qhd', probs, value_heads, precision=lax.Precision.HIGHEST)
        return mixture.reshape(QB, model_width)
    starts = jnp.arange(blocks, dtype=jnp.int32) * QB
    pieces = lax.map(jax.checkpoint(one_block), (queries.reshape(blocks, QB, model_width), starts))
    return pieces.reshape(row_count, model_width)

def cell_forward(tokens, qkv_weight, out_weight, ff_in_weight, ff_out_weight, biases, gains, length, generate):
    row_count, model_width = tokens.shape
    projected = matmul(tokens, qkv_weight)
    queries = low(low_back(projected[:, :model_width] + biases[0]))
    keys = low(low_back(projected[:, model_width:2 * model_width]))
    values = low(low_back(projected[:, 2 * model_width:] + biases[1]))
    attended = low(low_back(attend(queries, keys, values, length, generate)))
    branch = low_back(matmul(attended, out_weight) + biases[2])
    normed = layer_norm(tokens + branch, gains[0], biases[5])
    before = low_back(matmul(low(normed), ff_in_weight) + biases[3])
    activated = low(jax.nn.gelu(before, approximate=False))
    feed = low_back(matmul(activated, ff_out_weight) + biases[4])
    final = layer_norm(normed + feed, gains[1], biases[6])
    valid = (jnp.arange(row_count, dtype=jnp.int32) < length).astype(jnp.float32)
    return final * valid[:, None]

def reference(tokens, cotangent, lengths, generate, qkv_weight, out_weight, ff_in_weight, ff_out_weight, biases, gains):
    weights = tuple((w.astype(jnp.float32) for w in (qkv_weight, out_weight, ff_in_weight, ff_out_weight, biases, gains)))

    def one_cell(totals, inputs_cell):
        cell_tokens, cell_cot, length, cell_generate = inputs_cell

        def forward(value, *params):
            return cell_forward(value, *params, length, cell_generate)
        result, pull = jax.vjp(forward, cell_tokens.astype(jnp.float32), *weights)
        grads = pull(cell_cot.astype(jnp.float32))
        totals = tuple((t + g for t, g in zip(totals, grads[1:])))
        return (totals, (result.astype(jnp.bfloat16), grads[0]))
    start_totals = tuple((jnp.zeros_like(w) for w in weights))
    totals, (mixed, tokens_grad) = lax.scan(one_cell, start_totals, (tokens, cotangent, lengths, generate))
    qkv_grad, out_grad, ff_in_grad, ff_out_grad, biases_grad, gains_grad = tuple((t / CELLS for t in totals))
    return (mixed, tokens_grad, qkv_grad, out_grad, ff_in_grad, ff_out_grad, biases_grad, gains_grad)
```

```python
import functools

import jax
import jax.numpy as jnp
from jax import lax
from jax.experimental import pallas as pl
from jax.experimental.pallas import tpu as pltpu
from jax.sharding import PartitionSpec as P

F32, BF = jnp.float32, jnp.bfloat16
MESH = pl.DeviceIdType.MESH
HEADS = 8
EPS = 1e-5
CHUNK = 384
GROUP = 8


def dot(a, b):
    return jnp.dot(a, b, preferred_element_type=F32)


def dot_t(a, b):
    return lax.dot_general(a, b, (((1,), (1,)), ((), ())), preferred_element_type=F32)


def col_sum(v):
    return jnp.sum(v, axis=0, keepdims=True)


def norm(v):
    centred = v - jnp.mean(v, axis=1, keepdims=True)
    r = lax.rsqrt(jnp.mean(centred * centred, axis=1, keepdims=True) + EPS)
    return centred * r, r


def norm_back(g, xhat, r):
    g_mean = jnp.mean(g, axis=1, keepdims=True)
    x_mean = jnp.mean(g * xhat, axis=1, keepdims=True)
    return r * (g - g_mean - xhat * x_mean)


def aligned(value, step):
    return pl.multiple_of(value, step)


def layer_kernel(
    cells, fsdp, factor,
    len_ref, gen_ref, X, COT, wq_in, wo_in, w1_in, w2_in, bias_in, gain_in,
    mixed, tgrad, qkv_out, wo_out, w1_out, w2_out, bias_out, gain_out,
    W, VEC, XT, B, qp, km, VF, e, att, rL, A5, dAx, dkacc, dvacc, vecg,
    G, R1, H, S2, R2, P3, R3, R3b, R4, V0, VR1, V1, VR2, V2, VR3,
    in_sem, gs_sem, gr_sem, vs_sem, vr_sem,
    s1s, s1r, s2s, s2r, s3s, s3r, s3bs, s3br, s4s, s4r, v1s, v1r, v2s, v2r, v3s, v3r,
):
    rows_n, width = X.shape
    pairs = HEADS // 2
    act, gf, nl, gb, gbr = (A5.at[:, pl.ds(i * width, width)] for i in range(5))
    dqkv = A5.at[:, pl.ds(0, 3 * width)]
    QB = 256
    RB = 256
    blocks = rows_n // QB
    cell = lax.axis_index("cells")
    shard = lax.axis_index("fsdp")
    group = min(GROUP, cells)
    far = cells // group
    low = lax.rem(cell, group)
    high = lax.div(cell, group)

    def near_shard(s):
        return s + 1 - 2 * lax.rem(s, 2)

    def far_shard(s):
        return s + 2 - 4 * lax.rem(lax.div(s, 2), 2)

    def fsdp_dev(s):
        return (cell, s)

    def low_dev(r):
        return (high * group + lax.rem(low + r, group), shard)

    def high_dev(r):
        return (lax.rem(high + r, far) * group + low, shard)

    s_near, s_far = near_shard(shard), far_shard(shard)
    s_diag = near_shard(s_far)

    def remote(src, dst, send, recv, device):
        return pltpu.make_async_remote_copy(
            src_ref=src, dst_ref=dst, send_sem=send, recv_sem=recv, device_id=device, device_id_type=MESH
        )

    barrier = pltpu.get_barrier_semaphore()
    for s in (s_near, s_far, s_diag):
        pl.semaphore_signal(barrier, inc=1, device_id=fsdp_dev(s), device_id_type=MESH)
    for r in range(1, group):
        pl.semaphore_signal(barrier, inc=1, device_id=low_dev(r), device_id_type=MESH)
    for r in range(1, far):
        pl.semaphore_signal(barrier, inc=1, device_id=high_dev(r), device_id_type=MESH)

    own = pl.ds(aligned(shard * 128, 128), 128)
    loads = []
    for p in range(pairs):
        for t in range(3):
            loads.append((wq_in.at[:, pl.ds(t * width + p * 128, 128)], W.at[own, pl.ds(p * CHUNK + t * 128, 128)]))
    for i, ref in enumerate((wo_in, w1_in, w2_in)):
        loads.append((ref, W.at[own, pl.ds((3 + i) * width, width)]))
    loads = [pltpu.make_async_copy(a, b, in_sem.at[i]) for i, (a, b) in enumerate(loads)]
    for copy in loads:
        copy.start()
    VEC[shard] = jnp.zeros((16, 128), F32)
    VEC[shard, 0:7, :] = bias_in[...].astype(F32)
    VEC[shard, 8:10, :] = gain_in[...].astype(F32)
    pl.semaphore_wait(barrier, fsdp - 1 + group - 1 + far - 1)

    def w_copy(c, owner, hop, device):
        part = W.at[pl.ds(aligned(owner * 128, 128), 128), pl.ds(c * CHUNK, CHUNK)]
        return remote(part, part, gs_sem.at[c, hop], gr_sem.at[c, hop], device)

    def vec_copy(i, s):
        return remote(VEC.at[shard], VEC.at[shard], vs_sem.at[i], vr_sem.at[i], fsdp_dev(s))

    for i, s in enumerate((s_near, s_far, s_diag)):
        vec_copy(i, s).start()
    chunks = 8
    for c in range(chunks):
        if c < pairs:
            for t in range(3):
                loads[3 * c + t].wait()
        if c == pairs:
            for t in range(3):
                loads[3 * pairs + t].wait()
        w_copy(c, shard, 1, fsdp_dev(s_far)).start()
        w_copy(c, shard, 0, fsdp_dev(s_near)).start()

    def w_forward(c):
        w_copy(c, shard, 1, fsdp_dev(s_far)).wait_recv()
        w_copy(c, s_far, 2, fsdp_dev(s_near)).start()

    def w_ready(c):
        w_copy(c, shard, 0, fsdp_dev(s_near)).wait_recv()
        w_copy(c, s_far, 2, fsdp_dev(s_near)).wait_recv()

    length = len_ref[0]
    XT[...] = X[...].T
    col_ids = lax.broadcasted_iota(jnp.int32, (1, rows_n), 1)
    visible = jnp.where((col_ids < length) & (gen_ref[...] == 0), 0.0, -1e9).astype(F32)

    def mask_rows(i, _):
        r = aligned(i * 128, 128)
        row_ids = lax.broadcasted_iota(jnp.int32, (128, rows_n), 0) + r
        ids = lax.broadcasted_iota(jnp.int32, (128, rows_n), 1)
        B[pl.ds(r, 128), :] = jnp.where(row_ids == ids, 0.0, visible).astype(BF)
        return 0

    lax.fori_loop(0, rows_n // 128, mask_rows, 0)
    w_forward(0)
    for i, s in enumerate((s_near, s_far, s_diag)):
        vec_copy(i, s).wait_recv()
    w_ready(0)

    def bias_row(i):
        return jnp.concatenate([VEC[s, i : i + 1, :] for s in range(fsdp)], 1)

    def forward_pair(p, _):
        pr = dot(X[...], W[:, pl.ds(aligned(p * CHUNK, 128), CHUNK)])
        q = (pr[:, :128] + VEC[p, 0:1, :]).astype(BF) * jnp.asarray(0.125, BF)
        k = pr[:, 128:256].astype(BF)
        v = (pr[:, 256:] + VEC[p, 1:2, :]).astype(BF)
        first = lax.broadcasted_iota(jnp.int32, (rows_n, 128), 1) < 64
        zero, one = jnp.zeros_like(k), jnp.ones_like(k)
        qp[p] = q
        km[2 * p] = jnp.where(first, k, zero)
        km[2 * p + 1] = jnp.where(first, zero, k)
        VF[2 * p, :, 0:128] = jnp.where(first, v, zero)
        VF[2 * p, :, 128:256] = jnp.where(first, one, zero)
        VF[2 * p + 1, :, 0:128] = jnp.where(first, zero, v)
        VF[2 * p + 1, :, 128:256] = jnp.where(first, zero, one)

        def block(b, _):
            rows = pl.ds(aligned(b * QB, QB), QB)
            qb = qp[p, rows, :]
            o = None
            for h in range(2):
                s = dot_t(qb, km[2 * p + h]) + B[rows, :].astype(F32)
                weights = jnp.exp(s - jnp.max(s, axis=1, keepdims=True)).astype(BF)
                e[2 * p + h, rows, :] = weights
                part = dot(weights, VF[2 * p + h])
                o = part if o is None else o + part
            rl = 1.0 / o[:, 128:]
            att[rows, pl.ds(aligned(p * 128, 128), 128)] = (o[:, :128] * rl).astype(BF)
            rL[p, rows, :] = rl
            return 0

        for c in range(1, pairs):
            pl.when(p == c - 1)(functools.partial(w_forward, c))
        lax.fori_loop(0, blocks, block, 0)
        for c in range(1, pairs):
            pl.when(p == c - 1)(functools.partial(w_ready, c))
        return 0

    lax.fori_loop(0, pairs, forward_pair, 0)
    for c in range(pairs, chunks):
        w_forward(c)
    for c in range(pairs, chunks):
        w_ready(c)

    wo, w1, w2 = (pl.ds((3 + i) * width, width) for i in range(3))
    vecg[...] = jnp.zeros_like(vecg)

    def rows_step(i, _):
        r0 = aligned(i * RB, RB)
        rows = pl.ds(r0, RB)
        a = att[rows, :]
        gain0, gain1 = bias_row(8), bias_row(9)
        summed = X[rows, :].astype(F32) + dot(a, W[:, wo]) + bias_row(2)
        xh1, rs1 = norm(summed)
        normed = xh1 * gain0 + bias_row(5)
        n_low = normed.astype(BF)
        before = dot(n_low, W[:, w1]) + bias_row(3)
        cdf = 0.5 * (1.0 + lax.erf(before * (2.0**-0.5)))
        pdf = jnp.exp(-0.5 * before * before) * (2.0 * jnp.pi) ** -0.5
        a_low = (before * cdf).astype(BF)
        slope = cdf + before * pdf
        second = normed + dot(a_low, W[:, w2]) + bias_row(4)
        xh2, rs2 = norm(second)
        valid = (lax.broadcasted_iota(jnp.int32, (RB, 1), 0) + r0 < length).astype(F32)
        mixed[rows, :] = ((xh2 * gain1 + bias_row(6)) * valid).astype(BF)
        g = COT[rows, :].astype(F32) * valid
        g_second = norm_back(g * gain1, xh2, rs2)
        g_feed = g_second.astype(BF)
        g_before = (slope * dot_t(g_feed, W[:, w2])).astype(BF)
        g_normed = g_second + dot_t(g_before, W[:, w1])
        g_summed = norm_back(g_normed * gain0, xh1, rs1)
        g_branch = g_summed.astype(BF)
        g_att = dot_t(g_branch, W[:, wo]).astype(BF)
        act[rows, :] = a_low
        gf[rows, :] = g_feed
        nl[rows, :] = n_low
        gb[rows, :] = g_before
        gbr[rows, :] = g_branch
        tgrad[rows, :] = g_summed
        vecg[2:3, :] += col_sum(g_branch.astype(F32))
        vecg[3:4, :] += col_sum(g_before.astype(F32))
        vecg[4:5, :] += col_sum(g_feed.astype(F32))
        vecg[5:6, :] += col_sum(g_normed)
        vecg[6:7, :] += col_sum(g)
        vecg[8:9, :] += col_sum(g_normed * xh1)
        vecg[9:10, :] += col_sum(g * xh2)
        lane = lax.broadcasted_iota(jnp.int32, (RB, 128), 1)
        same = (lax.broadcasted_iota(jnp.int32, (256, 128), 0) % 128 < 64) == (
            lax.broadcasted_iota(jnp.int32, (256, 128), 1) < 64
        )
        head_ones = jnp.where(same, 1.0, 0.0).astype(BF)
        for p in range(pairs):
            cols = slice(128 * p, 128 * p + 128)
            ga = g_att[:, cols].astype(F32)
            prod = ga * a[:, cols].astype(F32)
            hi = prod.astype(BF)
            lo = (prod - hi.astype(F32)).astype(BF)
            rl = rL[p, rows, :]
            shift = -dot(jnp.concatenate([hi, lo], 1), head_ones) * rl
            s_hi = shift.astype(BF)
            s_lo = (shift - s_hi.astype(F32)).astype(BF)
            dAx[p, rows, 0:128] = (ga * rl).astype(BF)
            dAx[p, rows, 128:256] = jnp.where(
                lane % 64 == 0, s_hi, jnp.where(lane % 64 == 1, s_lo, jnp.zeros_like(s_hi))
            )
        return 0

    lax.fori_loop(0, rows_n // RB, rows_step, 0)

    def put_terms(c, term):
        term = (term * factor).astype(BF)
        for s in range(fsdp):
            G[c, s] = term[128 * s : 128 * s + 128, :]

    def s1_copy(c, i, s):
        return remote(G.at[c, s], R1.at[c, i], s1s.at[c, i], s1r.at[c, i], fsdp_dev(s_near))

    def s1_start(c):
        s1_copy(c, 0, s_near).start()
        s1_copy(c, 1, s_diag).start()

    def s2_copy(c):
        return remote(S2.at[c], R2.at[c], s2s.at[c], s2r.at[c], fsdp_dev(s_far))

    def s2_start(c):
        s1_copy(c, 0, s_near).wait_recv()
        s1_copy(c, 1, s_diag).wait_recv()
        S2[c] = (G[c, s_far].astype(F32) + R1[c, 1].astype(F32)).astype(BF)
        s2_copy(c).start()
        H[c] = G[c, shard].astype(F32) + R1[c, 0].astype(F32)

    piece = 128 // group

    def s3_copy(c, r):
        to = lax.rem(low + r, group)
        return remote(
            P3.at[c, pl.ds(aligned(to * piece, piece), piece)], R3.at[c, r - 1], s3s.at[c, r - 1], s3r.at[c, r - 1],
            low_dev(r),
        )

    def s3_start(c):
        s2_copy(c).wait_recv()
        P3[c] = (H[c] + R2[c].astype(F32)).astype(BF)
        for r in range(1, group):
            s3_copy(c, r).start()

    own_piece = pl.ds(aligned(low * piece, piece), piece)

    def s3b_copy(c, r):
        return remote(
            R4.at[c, own_piece], R3b.at[c, r - 1], s3bs.at[c, r - 1], s3br.at[c, r - 1], high_dev(r)
        )

    def s3b_start(c):
        total = P3[c, own_piece, :].astype(F32)
        for r in range(1, group):
            s3_copy(c, r).wait_recv()
            total = total + R3[c, r - 1].astype(F32)
        R4[c, own_piece, :] = total.astype(BF)
        for r in range(1, far):
            s3b_copy(c, r).start()

    def s4_copy(c, r):
        return remote(R4.at[c, own_piece], R4.at[c, own_piece], s4s.at[c, r - 1], s4r.at[c, r - 1], low_dev(r))

    def s4_start(c):
        if far > 1:
            total = R4[c, own_piece, :].astype(F32)
            for r in range(1, far):
                s3b_copy(c, r).wait_recv()
                total = total + R3b[c, r - 1].astype(F32)
            for r in range(1, far):
                s3b_copy(c, r).wait_send()
            R4[c, own_piece, :] = total.astype(BF)
        for r in range(1, group):
            s4_copy(c, r).start()

    def s3_end(c):
        s3b_start(c)
        s4_start(c)

    def s4_end(c):
        for r in range(1, group):
            s4_copy(c, r).wait_recv()

    def each(first, last, step):
        def run(c, _):
            step(c)
            return 0

        lax.fori_loop(first, last, run, 0)

    terms = [
        dot(att[...].T, gbr[...]),
        dot(nl[...].T, gb[...]),
        dot(act[...].T, gf[...]),
    ]
    for c in range(pairs):
        parts = []
        for j in range(3 * c, 3 * c + 3):
            parts.append(terms[j // 4][:, (j % 4) * 128 : (j % 4) * 128 + 128])
        put_terms(c, jnp.concatenate(parts, 1))
        s1_start(c)

    first_n = lax.broadcasted_iota(jnp.int32, (rows_n, 128), 1) < 64

    def backward_pair(p, _):
        def block(b, _):
            rows = pl.ds(aligned(b * QB, QB), QB)
            q = qp[p, rows, :]
            da = dAx[p, rows, :]
            dq, dk, dv = None, [], []
            for h in range(2):
                shifted = dot_t(da, VF[2 * p + h])
                weights = e[2 * p + h, rows, :]
                ds = (weights.astype(F32) * shifted).astype(BF)
                part = dot(ds, km[2 * p + h])
                dq = part if dq is None else dq + part
                dk.append(dot(ds.T, q))
                dv.append(dot(weights.T, da[:, :128]))
            dkk = jnp.where(first_n, dk[0], dk[1])
            dvv = jnp.where(first_n, dv[0], dv[1])

            @pl.when(b == 0)
            def _():
                dkacc[...] = dkk
                dvacc[...] = dvv

            @pl.when(b > 0)
            def _():
                dkacc[...] += dkk
                dvacc[...] += dvv

            dqkv[rows, pl.ds(aligned(p * CHUNK, 128), 128)] = (dq * 0.125).astype(BF)
            return 0

        lax.fori_loop(0, blocks, block, 0)
        c0 = aligned(p * CHUNK, 128)
        dqkv[:, pl.ds(c0 + 128, 128)] = dkacc[...].astype(BF)
        dqkv[:, pl.ds(c0 + 256, 128)] = dvacc[...].astype(BF)
        g = dqkv[:, pl.ds(c0, CHUNK)]
        c1 = aligned(p * 128, 128)
        vecg[0:1, pl.ds(c1, 128)] = col_sum(g[:, :128].astype(F32))
        vecg[1:2, pl.ds(c1, 128)] = col_sum(g[:, 256:].astype(F32))
        put_terms(pairs + p, dot(XT[...], g))
        s1_start(pairs + p)
        pl.when(p == 0)(functools.partial(each, 0, pairs, s2_start))
        pl.when(p == 1)(functools.partial(each, 0, pairs, s3_start))
        pl.when(p == 2)(functools.partial(each, 0, pairs, s3_end))
        pl.when(p >= 1)(lambda: s2_start(pairs + p - 1))
        pl.when(p >= 2)(lambda: s3_start(pairs + p - 2))
        pl.when(p >= 3)(lambda: s3_end(pairs + p - 3))
        return 0

    lax.fori_loop(0, pairs, backward_pair, 0)

    for s in range(fsdp):
        V0[s] = vecg[:, 128 * s : 128 * s + 128] * factor

    def v1_copy(i, s):
        return remote(V0.at[s], VR1.at[i], v1s.at[i], v1r.at[i], fsdp_dev(s))

    def v2_copy(r):
        return remote(V1, VR2.at[r - 1], v2s.at[r - 1], v2r.at[r - 1], low_dev(r))

    def v3_copy(r):
        return remote(V2, VR3.at[r - 1], v3s.at[r - 1], v3r.at[r - 1], high_dev(r))

    others = (s_near, s_far, s_diag)
    for i, s in enumerate(others):
        v1_copy(i, s).start()
    last = 2 * pairs - 1
    s2_start(last)
    s3_start(last - 1)
    s3_end(last - 2)

    def tokens_step(i, _):
        rows = pl.ds(aligned(i * RB, RB), RB)
        tgrad[rows, :] += dot_t(dqkv[rows, :], W[:, 0 : 3 * width])
        return 0

    lax.fori_loop(0, rows_n // RB, tokens_step, 0)
    s3_start(last)
    for i, s in enumerate(others):
        v1_copy(i, s).wait_recv()
    V1[...] = V0[shard] + VR1[0] + VR1[1] + VR1[2]
    for r in range(1, group):
        v2_copy(r).start()
    s3_end(last - 1)
    s3_end(last)
    total = V1[...]
    for r in range(1, group):
        v2_copy(r).wait_recv()
        total = total + VR2[r - 1]
    V2[...] = total
    for r in range(1, far):
        v3_copy(r).start()
    for r in range(1, far):
        v3_copy(r).wait_recv()
        total = total + VR3[r - 1]
    bias_out[...] = total[0:7, :]
    gain_out[...] = total[8:10, :]

    each(0, 2 * pairs, s4_end)
    for p in range(pairs):
        g = R4[pairs + p].astype(F32)
        for t in range(3):
            qkv_out[:, t * width + p * 128 : t * width + p * 128 + 128] = g[:, 128 * t : 128 * t + 128]
        g = R4[p].astype(F32)
        for t in range(3):
            j = 3 * p + t
            (wo_out, w1_out, w2_out)[j // 4][:, (j % 4) * 128 : (j % 4) * 128 + 128] = g[:, 128 * t : 128 * t + 128]

    for c in range(chunks):
        w_copy(c, shard, 1, fsdp_dev(s_far)).wait_send()
        w_copy(c, shard, 0, fsdp_dev(s_near)).wait_send()
        w_copy(c, s_far, 2, fsdp_dev(s_near)).wait_send()

    def drain(c):
        s1_copy(c, 0, s_near).wait_send()
        s1_copy(c, 1, s_diag).wait_send()
        s2_copy(c).wait_send()
        for r in range(1, group):
            s3_copy(c, r).wait_send()
            s4_copy(c, r).wait_send()

    each(0, 2 * pairs, drain)
    for i, s in enumerate(others):
        vec_copy(i, s).wait_send()
        v1_copy(i, s).wait_send()
    for r in range(1, group):
        v2_copy(r).wait_send()
    for r in range(1, far):
        v3_copy(r).wait_send()


def call_layer(cells, fsdp, rows_n, width, *args):
    vm = pl.BlockSpec(memory_space=pltpu.VMEM)
    sm = pl.BlockSpec(memory_space=pltpu.SMEM)
    shard_rows = width // fsdp
    group = min(GROUP, cells)
    far = cells // group
    piece = 128 // group
    chunks = 8
    factor = 1.0 / (cells * fsdp)
    dma = pltpu.SemaphoreType.DMA
    outs = (
        ((rows_n, width), BF), ((rows_n, width), F32), ((shard_rows, 3 * width), F32), ((shard_rows, width), F32),
        ((shard_rows, width), F32), ((shard_rows, width), F32), ((7, width // fsdp), F32), ((2, width // fsdp), F32),
    )
    far_n = max(far - 1, 1)
    scratch = [
        ((width, 6 * width), BF), ((fsdp, 16, 128), F32), ((width, rows_n), BF), ((rows_n, rows_n), BF),
        ((4, rows_n, 128), BF), ((8, rows_n, 128), BF), ((8, rows_n, 256), BF), ((8, rows_n, rows_n), BF),
        ((rows_n, width), BF), ((4, rows_n, 128), F32), ((rows_n, 5 * width), BF),
        ((4, rows_n, 256), BF), ((rows_n, 128), F32), ((rows_n, 128), F32), ((16, width), F32),
        ((chunks, fsdp, 128, CHUNK), BF), ((chunks, 2, 128, CHUNK), BF), ((chunks, 128, CHUNK), F32),
        ((chunks, 128, CHUNK), BF), ((chunks, 128, CHUNK), BF), ((chunks, 128, CHUNK), BF),
        ((chunks, group - 1, piece, CHUNK), BF), ((chunks, far_n, piece, CHUNK), BF), ((chunks, 128, CHUNK), BF),
        ((fsdp, 16, 128), F32), ((fsdp - 1, 16, 128), F32), ((16, 128), F32), ((group - 1, 16, 128), F32),
        ((16, 128), F32), ((far_n, 16, 128), F32),
    ]
    sems = [
        (15,), (chunks, 3), (chunks, 3), (3,), (3,),
        (chunks, 2), (chunks, 2), (chunks,), (chunks,), (chunks, group - 1), (chunks, group - 1), (chunks, far_n),
        (chunks, far_n), (chunks, group - 1), (chunks, group - 1), (3,), (3,), (group - 1,), (group - 1,), (far_n,),
        (far_n,),
    ]
    return pl.pallas_call(
        functools.partial(layer_kernel, cells, fsdp, factor),
        out_shape=[jax.ShapeDtypeStruct(s, t) for s, t in outs],
        in_specs=[sm] + [vm] * 9,
        out_specs=[vm] * 8,
        scratch_shapes=[pltpu.VMEM(s, t) for s, t in scratch] + [dma(s) for s in sems],
        compiler_params=pltpu.CompilerParams(
            vmem_limit_bytes=63 * 2**20, collective_id=0, has_side_effects=True
        ),
        name="layer",
    )(*args)


def body(cells, fsdp, tokens, cotangent, lengths, generate, *weights):
    _, rows_n, width = tokens.shape
    mixed, tokens_grad, *grads = call_layer(
        cells, fsdp, rows_n, width, lengths, generate, tokens[0], cotangent[0], *weights
    )
    return (mixed[None], tokens_grad[None], *grads)


def solution(mesh):
    split = P(("cells", "fsdp"), None, None)
    rows, cols = P("fsdp", None), P(None, "fsdp")
    return jax.shard_map(
        functools.partial(body, mesh.shape["cells"], mesh.shape["fsdp"]),
        mesh=mesh,
        in_specs=(split, split, P(("cells", "fsdp")), P(("cells", "fsdp"), None), rows, rows, rows, rows, cols, cols),
        out_specs=(split, split, rows, rows, rows, rows, cols, cols),
        check_vma=False,
    )
```

```python
import functools

import jax
import jax.numpy as jnp
from jax import lax
from jax.experimental import pallas as pl
from jax.experimental.pallas import tpu as pltpu
from jax.sharding import PartitionSpec as P

F32, BF = jnp.float32, jnp.bfloat16
MESH = pl.DeviceIdType.MESH
HEADS = 8
EPS = 1e-5
CHUNK = 384
GROUP = 8


def dot(a, b):
    return jnp.dot(a, b, preferred_element_type=F32)


def dot_t(a, b):
    return lax.dot_general(a, b, (((1,), (1,)), ((), ())), preferred_element_type=F32)


def col_sum(v):
    return jnp.sum(v, axis=0, keepdims=True)


def norm(v):
    centred = v - jnp.mean(v, axis=1, keepdims=True)
    r = lax.rsqrt(jnp.mean(centred * centred, axis=1, keepdims=True) + EPS)
    return centred * r, r


def norm_back(g, xhat, r):
    g_mean = jnp.mean(g, axis=1, keepdims=True)
    x_mean = jnp.mean(g * xhat, axis=1, keepdims=True)
    return r * (g - g_mean - xhat * x_mean)


def aligned(value, step):
    return pl.multiple_of(value, step)


def layer_kernel(
    cells, fsdp, factor,
    len_ref, gen_in, tok_in, cot_in, wq_in, wo_in, w1_in, w2_in, bias_in, gain_in,
    mixed_out, tgrad_out, sums_out, vec_out,
    X, COT, GEN, W, VEC, XT, BT, qp, QTz, KN, KT, VN, VT1, e, att, OT, rL, A5, dAn, dl, Z0, Z1, dQT,
    s0, s1, m0, m1, eb0, eb1, vecg,
    G, R1, R2, R3, R3b, R4, V0, VR1, V1, VR2, V2, VR3,
    in_sem, out_sem, gs_sem, gr_sem, vs_sem, vr_sem,
    s1s, s1r, s2s, s2r, s3s, s3r, s3bs, s3br, s4s, s4r, v1s, v1r, v2s, v2r, v3s, v3r,
):
    rows_n, width = X.shape
    pairs = HEADS // 2
    RB = 256
    LB = 256
    cell = lax.axis_index("cells")
    shard = lax.axis_index("fsdp")
    group = min(GROUP, cells)
    far = cells // group
    low = lax.rem(cell, group)
    high = lax.div(cell, group)
    act, gf, nl, gb, gbr = (A5.at[:, pl.ds(i * width, width)] for i in range(5))
    dATz, mixed, tgrad = QTz, COT, BT.at[:, pl.ds(0, width)]

    def near_shard(s):
        return s + 1 - 2 * lax.rem(s, 2)

    def far_shard(s):
        return s + 2 - 4 * lax.rem(lax.div(s, 2), 2)

    def fsdp_dev(s):
        return (cell, s)

    def low_dev(r):
        return (high * group + lax.rem(low + r, group), shard)

    def high_dev(r):
        return (lax.rem(high + r, far) * group + low, shard)

    s_near, s_far = near_shard(shard), far_shard(shard)
    s_diag = near_shard(s_far)
    others = (s_near, s_far, s_diag)

    def remote(src, dst, send, recv, device):
        return pltpu.make_async_remote_copy(
            src_ref=src, dst_ref=dst, send_sem=send, recv_sem=recv, device_id=device, device_id_type=MESH
        )

    barrier = pltpu.get_barrier_semaphore()
    for s in others:
        pl.semaphore_signal(barrier, inc=1, device_id=fsdp_dev(s), device_id_type=MESH)
    for r in range(1, group):
        pl.semaphore_signal(barrier, inc=1, device_id=low_dev(r), device_id_type=MESH)
    for r in range(1, far):
        pl.semaphore_signal(barrier, inc=1, device_id=high_dev(r), device_id_type=MESH)

    own = pl.ds(aligned(shard * 128, 128), 128)
    loads = []
    for p in range(pairs):
        for t in range(3):
            loads.append((wq_in.at[:, pl.ds(t * width + p * 128, 128)], W.at[own, pl.ds(p * CHUNK + t * 128, 128)]))
    for i, ref in enumerate((wo_in, w1_in, w2_in)):
        loads.append((ref, W.at[own, pl.ds((3 + i) * width, width)]))
    loads += [(tok_in, X), (gen_in, GEN), (cot_in, COT)]
    loads = [pltpu.make_async_copy(a, b, in_sem.at[i]) for i, (a, b) in enumerate(loads)]
    for copy in loads:
        copy.start()
    VEC[shard] = jnp.zeros((16, 128), F32)
    VEC[shard, 0:7, :] = bias_in[...].astype(F32)
    VEC[shard, 8:10, :] = gain_in[...].astype(F32)

    def w_copy(c, owner, hop, device):
        cols = pl.ds(c * CHUNK, CHUNK) if c < pairs else pl.ds(3 * width, 3 * width)
        part = W.at[pl.ds(aligned(owner * 128, 128), 128), cols]
        return remote(part, part, gs_sem.at[c, hop], gr_sem.at[c, hop], device)

    def vec_copy(i, s):
        return remote(VEC.at[shard], VEC.at[shard], vs_sem.at[i], vr_sem.at[i], fsdp_dev(s))

    parts = pairs + 1

    def w_send(c):
        w_copy(c, shard, 1, fsdp_dev(s_far)).start()
        w_copy(c, shard, 0, fsdp_dev(s_near)).start()

    def w_forward(c):
        w_copy(c, shard, 1, fsdp_dev(s_far)).wait_recv()
        w_copy(c, s_far, 2, fsdp_dev(s_near)).start()

    def w_ready(c):
        w_copy(c, shard, 0, fsdp_dev(s_near)).wait_recv()
        w_copy(c, s_far, 2, fsdp_dev(s_near)).wait_recv()

    for t in range(3):
        loads[t].wait()
    pl.semaphore_wait(barrier, fsdp - 1 + group - 1 + far - 1)
    w_send(0)
    for i, s in enumerate(others):
        vec_copy(i, s).start()
    for t in range(3, 6):
        loads[t].wait()
    w_send(1)

    length = len_ref[0]
    loads[3 * pairs + 3].wait()
    loads[3 * pairs + 4].wait()
    XT[...] = X[...].T
    col_ids = lax.broadcasted_iota(jnp.int32, (1, rows_n), 1)
    visible = jnp.where((col_ids < length) & (GEN[...] == 0), 0.0, -1e9).astype(F32)
    visible = jnp.broadcast_to(visible, (8, rows_n)).T[:, 0:1]

    def mask_cols(i, _):
        c = aligned(i * 128, 128)
        keys = lax.broadcasted_iota(jnp.int32, (rows_n, 128), 0)
        queries = lax.broadcasted_iota(jnp.int32, (rows_n, 128), 1) + c
        BT[:, pl.ds(c, 128)] = jnp.where(keys == queries, 0.0, visible)
        return 0

    lax.fori_loop(0, rows_n // 128, mask_cols, 0)
    QTz[...] = jnp.zeros_like(QTz)
    VT1[...] = jnp.ones_like(VT1)
    for t in range(6, 15):
        loads[t].wait()
    w_forward(0)
    w_send(2)
    w_send(3)
    for i, s in enumerate(others):
        vec_copy(i, s).wait_recv()
    w_ready(0)

    def bias_row(i):
        return jnp.concatenate([VEC[s, i : i + 1, :] for s in range(fsdp)], 1)

    def project(p, part):
        base = p * CHUNK
        if part == 0:
            pr = dot(X[...], W[:, pl.ds(aligned(base, 128), 256)])
            q = (pr[:, :128] + VEC[p, 0:1, :]).astype(BF) * jnp.asarray(0.125, BF)
            qp[p] = q
            KN[p] = pr[:, 128:256].astype(BF)
        if part == 1:
            pr = dot(X[...], W[:, pl.ds(aligned(base + 256, 128), 128)])
            VN[p] = (pr + VEC[p, 1:2, :]).astype(BF)
            qt = qp[p].T
            QTz[2 * p, 0:64, :] = qt[0:64]
            QTz[2 * p + 1, 64:128, :] = qt[64:128]
        if part == 2:
            KT[p] = KN[p].T
            vt = VN[p].T
            VT1[2 * p, 0:64, :] = vt[0:64]
            VT1[2 * p + 1, 0:64, :] = vt[64:128]

    units = HEADS * (rows_n // LB)
    per_head = rows_n // LB
    per_pair = 2 * per_head

    def unit(u):
        return u // per_head, u // per_pair, pl.ds(aligned((u % per_head) * LB, LB), LB)

    def score(u, s_ref, m_ref):
        h, p, cols = unit(jnp.minimum(u, units - 1))
        s = dot(KN[p], QTz[h, :, cols]) + BT[:, cols]
        s_ref[...] = s
        m_ref[0:1, :] = jnp.max(s, axis=0, keepdims=True)

    def weigh(u, s_ref, m_ref, e_ref):
        h, p, cols = unit(u)
        v = jnp.exp(s_ref[...] - m_ref[0:1, :]).astype(BF)
        e[h, :, cols] = v
        e_ref[...] = v

    def mix(u, e_ref):
        h, p, cols = unit(jnp.maximum(u, 0))
        o = dot(VT1[h], e_ref[...])
        r = 1.0 / o[64:65, :]
        rL[h, 0:1, cols] = r
        OT[h, :, cols] = o[0:64, :] * r

    slots = ((s0, m0, s1, m1, eb0, eb1), (s1, m1, s0, m0, eb1, eb0))
    for i in range(3):
        project(0, i)
    score(0, s0, m0)

    def forward_pair(p, is_last):
        for c in range(1, pairs):
            pl.when(p == c - 1)(functools.partial(w_forward, c))
        for n in range(per_pair):
            sa, ma, sb, mb, ea, eb = slots[n % 2]
            if n == 4:
                for c in range(1, pairs):
                    pl.when(p == c - 1)(functools.partial(w_ready, c))
                pl.when(p == 0)(functools.partial(w_send, pairs))
                if is_last:
                    w_forward(pairs)
            if not is_last and 4 <= n < 7:
                project(p + 1, n - 4)
            u = per_pair * p + n
            score(u + 1, sb, mb)
            weigh(u, sa, ma, ea)
            mix(u - 1, eb)
        return 0

    lax.fori_loop(0, pairs - 1, lambda p, _: forward_pair(p, False), 0)
    forward_pair(pairs - 1, True)
    mix(units - 1, slots[(per_pair - 1) % 2][4])
    for p in range(pairs):
        ot = jnp.concatenate([OT[2 * p], OT[2 * p + 1]], 0).astype(BF)
        att[:, 128 * p : 128 * p + 128] = ot.T
    w_ready(pairs)
    loads[3 * pairs + 5].wait()

    wo, w1, w2 = (pl.ds((3 + i) * width, width) for i in range(3))
    vecg[...] = jnp.zeros_like(vecg)

    def rows_step(i, _):
        r0 = aligned(i * RB, RB)
        rows = pl.ds(r0, RB)
        gain0, gain1 = bias_row(8), bias_row(9)
        summed = X[rows, :].astype(F32) + dot(att[rows, :], W[:, wo]) + bias_row(2)
        xh1, rs1 = norm(summed)
        normed = xh1 * gain0 + bias_row(5)
        n_low = normed.astype(BF)
        before = dot(n_low, W[:, w1]) + bias_row(3)
        cdf = 0.5 * (1.0 + lax.erf(before * (2.0**-0.5)))
        pdf = jnp.exp(-0.5 * before * before) * (2.0 * jnp.pi) ** -0.5
        a_low = (before * cdf).astype(BF)
        slope = cdf + before * pdf
        second = normed + dot(a_low, W[:, w2]) + bias_row(4)
        xh2, rs2 = norm(second)
        valid = (lax.broadcasted_iota(jnp.int32, (RB, 1), 0) + r0 < length).astype(F32)
        g = COT[rows, :].astype(F32) * valid
        mixed[rows, :] = ((xh2 * gain1 + bias_row(6)) * valid).astype(BF)
        g_second = norm_back(g * gain1, xh2, rs2)
        g_feed = g_second.astype(BF)
        g_before = (slope * dot_t(g_feed, W[:, w2])).astype(BF)
        g_normed = g_second + dot_t(g_before, W[:, w1])
        g_summed = norm_back(g_normed * gain0, xh1, rs1)
        g_branch = g_summed.astype(BF)
        g_att = dot_t(g_branch, W[:, wo]).astype(BF)
        act[rows, :] = a_low
        gf[rows, :] = g_feed
        nl[rows, :] = n_low
        gb[rows, :] = g_before
        gbr[rows, :] = g_branch
        tgrad[rows, :] = g_summed
        vecg[2:3, :] += col_sum(g_branch.astype(F32))
        vecg[3:4, :] += col_sum(g_before.astype(F32))
        vecg[4:5, :] += col_sum(g_feed.astype(F32))
        vecg[5:6, :] += col_sum(g_normed)
        vecg[6:7, :] += col_sum(g)
        vecg[8:9, :] += col_sum(g_normed * xh1)
        vecg[9:10, :] += col_sum(g * xh2)
        for p in range(pairs):
            dAn[p, rows, :] = g_att[:, 128 * p : 128 * p + 128]
        return 0

    lax.fori_loop(0, rows_n // RB, rows_step, 0)
    mixed_copy = pltpu.make_async_copy(mixed, mixed_out, out_sem.at[0])
    mixed_copy.start()

    near, stride = min(2, group), max(group // 2, 1)
    side, place = lax.rem(low, near), lax.div(low, near)
    band = 128 // near
    piece = band // stride
    own_rows = pl.ds(aligned(side * band + place * piece, piece), piece)

    def cell_dev(side_to, place_to, s):
        return (high * group + lax.rem(place_to, stride) * near + side_to, s)

    def cols_of(c):
        if isinstance(c, tuple):
            return 4 + c[0], pl.ds(aligned(4 * width + c[0] * 256, 256), 256)
        return c, pl.ds(c * width, width)

    def s1_all(c):
        i, cols = cols_of(c)
        return [
            remote(G.at[s, :, cols], R1.at[k, :, cols], s1s.at[i, k], s1r.at[i, k], fsdp_dev(s_near))
            for k, s in enumerate((s_near, s_diag))
        ]

    def s1_start(c):
        for copy in s1_all(c):
            copy.start()

    def s2_all(c):
        i, cols = cols_of(c)
        mine = pl.ds(aligned(side * band, band), band)
        other = pl.ds(aligned((near - 1 - side) * band, band), band)
        to = near - 1 - side
        plan = [(s_far, mine, side, s_far)]
        if near > 1:
            plan += [(shard, other, to, shard), (s_far, other, to, s_far)]
        return [
            remote(G.at[s, rows, cols], R2.at[k, :, cols], s2s.at[i, k], s2r.at[i, k], cell_dev(to_side, place, s))
            for k, (s, rows, to_side, _) in enumerate(plan)
        ]

    def s2_start(c):
        i, cols = cols_of(c)
        for copy in s1_all(c):
            copy.wait_recv()
        G[s_far, :, cols] = (G[s_far, :, cols].astype(F32) + R1[1, :, cols].astype(F32)).astype(BF)
        G[shard, :, cols] = (G[shard, :, cols].astype(F32) + R1[0, :, cols].astype(F32)).astype(BF)
        for copy in s2_all(c):
            copy.start()

    def s3_one(c, r):
        i, cols = cols_of(c)
        to = lax.rem(place + r, stride)
        rows = pl.ds(aligned(side * band + to * piece, piece), piece)
        return remote(
            G.at[shard, rows, cols], R3.at[r - 1, :, cols], s3s.at[i], s3r.at[i], cell_dev(side, place + r, shard)
        )

    def s3_whole(c):
        i, cols = cols_of(c)
        part = R3.at[:, :, cols]
        return remote(part, part, s3s.at[i], s3r.at[i], cell_dev(side, place + 1, shard))

    def s3_start(c):
        i, cols = cols_of(c)
        mine = pl.ds(aligned(side * band, band), band)
        total = G[shard, mine, cols].astype(F32)
        for k, copy in enumerate(s2_all(c)):
            copy.wait_recv()
            total = total + R2[k, :, cols].astype(F32)
        G[shard, mine, cols] = total.astype(BF)
        for r in range(1, stride):
            s3_one(c, r).start()

    def far_one(c, r):
        i, cols = cols_of(c)
        return remote(R4.at[own_rows, cols], R3b.at[r - 1, :, cols], s3bs.at[i, r - 1], s3br.at[i, r - 1], high_dev(r))

    def s4_one(c, r):
        i, cols = cols_of(c)
        part = R4.at[own_rows, cols]
        return remote(part, part, s4s.at[i], s4r.at[i], low_dev(r))

    def s4_whole(c):
        i, cols = cols_of(c)
        part = R4.at[pl.ds(0, 128 - piece), cols]
        return remote(part, part, s4s.at[i], s4r.at[i], low_dev(1))

    def s4_start(c):
        i, cols = cols_of(c)
        total = G[shard, own_rows, cols].astype(F32)
        s3_whole(c).wait_recv()
        for r in range(1, stride):
            total = total + R3[r - 1, :, cols].astype(F32)
        R4[own_rows, cols] = total.astype(BF)
        if far > 1:
            for r in range(1, far):
                far_one(c, r).start()
            for r in range(1, far):
                far_one(c, r).wait_recv()
                total = total + R3b[r - 1, :, cols].astype(F32)
            for r in range(1, far):
                far_one(c, r).wait_send()
            R4[own_rows, cols] = total.astype(BF)
        for r in range(1, group):
            s4_one(c, r).start()

    def drain(c):
        for copy in s1_all(c) + s2_all(c):
            copy.wait_send()
        s3_whole(c).wait_send()
        s4_whole(c).wait_send()

    def each_pair(step):
        def run(p, _):
            step((p,))
            return 0

        lax.fori_loop(0, pairs, run, 0)

    for i, (left, right) in enumerate(((att, gbr), (nl, gb), (act, gf))):
        term = (dot(left[...].T, right[...]) * factor).astype(BF)
        for s in range(fsdp):
            G[s, :, width * i : width * i + width] = term[128 * s : 128 * s + 128, :]
        s1_start(i)
    s2_start(0)
    s2_start(1)

    def prepare(p, _):
        gt = dAn[p].T.astype(F32)
        parts = []
        for hh in range(2):
            h = 2 * p + hh
            x = (gt[64 * hh : 64 * hh + 64, :] * rL[h, 0:1, :]).astype(BF)
            dl[h, 0:1, :] = col_sum(x.astype(F32) * OT[h])
            dATz[h, 64 * hh : 64 * hh + 64, :] = x
            parts.append(x)
        dAn[p] = jnp.concatenate(parts, 0).T
        return 0

    lax.fori_loop(0, pairs, prepare, 0)
    s2_start(2)

    def score_grads(p, hh, n, z_ref):
        cols = pl.ds(n * LB, LB)
        h = 2 * p + hh
        shifted = dot(VN[p], dATz[h, :, cols]) - dl[h, 0:1, cols]
        z_ref[:, cols] = (shifted * e[h, :, cols].astype(F32)).astype(BF)

    def query_grads(p, hh, n, z_ref):
        cols = pl.ds(n * LB, LB)
        half = slice(64 * hh, 64 * hh + 64)
        dQT[p, half, cols] = (dot(KT[p, half, :], z_ref[:, cols]) * 0.125).astype(BF)

    first = lax.broadcasted_iota(jnp.int32, (LB, 128), 1) < 64
    dka = s0.at[:, pl.ds(0, 128)]

    def value_grads(p, _):
        cols = pl.ds(aligned(p * CHUNK + 256, 128), 128)
        for n in range(per_head):
            rows = pl.ds(n * LB, LB)
            dv0 = dot(e[2 * p, rows, :], dAn[p])
            dv1 = dot(e[2 * p + 1, rows, :], dAn[p])
            A5[rows, cols] = jnp.where(first, dv0, dv1).astype(BF)
        return 0

    def key_grads(p, hh, n, z_ref):
        rows = pl.ds(n * LB, LB)
        dk = dot(z_ref[rows, :], qp[p])
        if hh == 0:
            dka[rows, :] = dk
        else:
            c = aligned(p * CHUNK, 128)
            A5[rows, pl.ds(c + 128, 128)] = jnp.where(first, dka[rows, :], dk).astype(BF)

    def put_term(n, cols, source):
        G[n, :, cols] = (dot(XT[128 * n : 128 * n + 128, :], source) * factor).astype(BF)

    def pair_term(p, n):
        source = A5[:, pl.ds(aligned(p * CHUNK, 128), 256)]
        put_term(n, pl.ds(aligned(4 * width + p * 256, 256), 256), source)

    def pair_end(p):
        c = aligned(p * CHUNK, 128)
        A5[:, pl.ds(c, 128)] = dQT[p].T
        vecg[0:1, pl.ds(aligned(p * 128, 128), 128)] = col_sum(A5[:, pl.ds(c, 128)].astype(F32))

    lax.fori_loop(0, pairs, value_grads, 0)
    s3_start(0)
    all_dv = jnp.concatenate([A5[:, CHUNK * p + 256 : CHUNK * p + 384] for p in range(pairs)], 1)
    put = (dot(XT[...], all_dv) * factor).astype(BF)
    for n in range(fsdp):
        G[n, :, 3 * width : 4 * width] = put[128 * n : 128 * n + 128, :]
    s1_start(3)
    vecg[1:2, :] = col_sum(all_dv.astype(F32))

    def backward_pair(p, _):
        before = jnp.maximum(p - 1, 0)
        for n in range(per_head):
            key_grads(before, 1, n, Z1)
            if n == 0:
                query_grads(before, 1, per_head - 1, Z1)
            else:
                query_grads(p, 0, n - 1, Z0)
            score_grads(p, 0, n, Z0)
        pair_end(before)
        pl.when(p == 0)(lambda: s2_start(3))
        pl.when(p == 1)(lambda: s3_start(2))
        pl.when(p == 2)(lambda: s3_start(3))
        pl.when(p >= 2)(lambda: s2_start((p - 2,)))
        pl.when(p == 3)(lambda: s3_start((0,)))
        for n in range(per_head):
            key_grads(p, 0, n, Z0)
            if n == 0:
                query_grads(p, 0, per_head - 1, Z0)
            else:
                query_grads(p, 1, n - 1, Z1)
            score_grads(p, 1, n, Z1)
            pair_term(before, n)
        pl.when(p >= 1)(lambda: s1_start((p - 1,)))
        pl.when(p == 0)(lambda: s3_start(1))
        pl.when(p == 0)(lambda: s4_start(0))
        pl.when(p == 1)(lambda: s4_start(1))
        pl.when(p == 2)(lambda: s4_start(2))
        pl.when(p == 3)(lambda: s4_start(3))
        return 0

    lax.fori_loop(0, pairs, backward_pair, 0)
    last = pairs - 1
    for n in range(per_head):
        key_grads(last, 1, n, Z1)
    query_grads(last, 1, per_head - 1, Z1)
    pair_end(last)
    s2_start((2,))
    for n in range(per_head):
        pair_term(last, n)
    s1_start((3,))

    for s in range(fsdp):
        V0[s] = vecg[:, 128 * s : 128 * s + 128] * factor

    def v1_copy(i, s):
        return remote(V0.at[s], VR1.at[i], v1s.at[i], v1r.at[i], fsdp_dev(s))

    def v2_copy(r):
        return remote(V1, VR2.at[r - 1], v2s.at[r - 1], v2r.at[r - 1], low_dev(r))

    def v3_copy(r):
        return remote(V2, VR3.at[r - 1], v3s.at[r - 1], v3r.at[r - 1], high_dev(r))

    for i, s in enumerate(others):
        v1_copy(i, s).start()
    s3_start((1,))
    s4_start((0,))
    s2_start((3,))

    def tokens_step(i, _):
        rows = pl.ds(aligned(i * RB, RB), RB)
        tgrad[rows, :] += dot_t(A5[rows, 0 : 3 * width], W[:, 0 : 3 * width])
        return 0

    lax.fori_loop(0, rows_n // RB, tokens_step, 0)
    tgrad_copy = pltpu.make_async_copy(tgrad, tgrad_out, out_sem.at[1])
    tgrad_copy.start()
    for i, s in enumerate(others):
        v1_copy(i, s).wait_recv()
    V1[...] = V0[shard] + VR1[0] + VR1[1] + VR1[2]
    for r in range(1, group):
        v2_copy(r).start()
    s3_start((2,))
    s4_start((1,))
    s3_start((3,))
    s4_start((2,))
    total = V1[...]
    for r in range(1, group):
        v2_copy(r).wait_recv()
        total = total + VR2[r - 1]
    if far > 1:
        V2[...] = total
        for r in range(1, far):
            v3_copy(r).start()
        for r in range(1, far):
            v3_copy(r).wait_recv()
            total = total + VR3[r - 1]
    VR1[0] = total
    vec_end = pltpu.make_async_copy(VR1.at[0], vec_out, out_sem.at[2])
    vec_end.start()
    s4_start((3,))
    for c in range(4):
        s4_whole(c).wait_recv()
    each_pair(lambda c: s4_whole(c).wait_recv())
    sums_copy = pltpu.make_async_copy(R4, sums_out, out_sem.at[3])
    sums_copy.start()

    for c in range(parts):
        w_copy(c, shard, 1, fsdp_dev(s_far)).wait_send()
        w_copy(c, shard, 0, fsdp_dev(s_near)).wait_send()
        w_copy(c, s_far, 2, fsdp_dev(s_near)).wait_send()

    for c in range(4):
        drain(c)
    each_pair(drain)
    for i, s in enumerate(others):
        vec_copy(i, s).wait_send()
        v1_copy(i, s).wait_send()
    for r in range(1, group):
        v2_copy(r).wait_send()
    for r in range(1, far):
        v3_copy(r).wait_send()
    for copy in (mixed_copy, tgrad_copy, vec_end, sums_copy):
        copy.wait()


def finish_kernel(
    mixed_in, tgrad_in, sums_in, vec_in, mixed_out, tgrad_out, qkv_out, wo_out, w1_out, w2_out, bias_out, gain_out,
    M, T, R, V, Q, O, A, B, bias, gain, sem,
):
    width = M.shape[1]
    pairs = HEADS // 2
    steps = 4
    rows = M.shape[0] // steps
    ins, outs = [], []

    def start(src, dst):
        copy = pltpu.make_async_copy(src, dst, sem.at[len(ins) + len(outs)])
        copy.start()
        return copy

    for i in range(steps):
        part = pl.ds(i * rows, rows)
        ins.append(start(tgrad_in.at[part], T.at[part]))
        ins.append(start(mixed_in.at[part], M.at[part]))
    ins.append(start(sums_in, R))
    ins.append(start(vec_in, V))
    for i in range(steps):
        part = pl.ds(i * rows, rows)
        ins[2 * i].wait()
        outs.append(start(T.at[part], tgrad_out.at[part]))
        ins[2 * i + 1].wait()
        outs.append(start(M.at[part], mixed_out.at[part]))
    ins[2 * steps].wait()
    for p in range(pairs):
        for t in range(2):
            c = 4 * width + 256 * p + 128 * t
            Q[:, t * width + p * 128 : t * width + p * 128 + 128] = R[:, c : c + 128].astype(F32)
    Q[:, 2 * width :] = R[:, 3 * width : 4 * width].astype(F32)
    outs.append(start(Q, qkv_out))
    for i, ref in enumerate((O, A, B)):
        ref[...] = R[:, i * width : i * width + width].astype(F32)
    for src, dst in ((O, wo_out), (A, w1_out), (B, w2_out)):
        outs.append(start(src, dst))
    ins[2 * steps + 1].wait()
    bias[...] = V[0:7, :]
    gain[...] = V[8:10, :]
    outs.append(start(bias, bias_out))
    outs.append(start(gain, gain_out))
    for copy in outs:
        copy.wait()


def call_layer(cells, fsdp, rows_n, width, lengths, generate, *args):
    vm = pl.BlockSpec(memory_space=pltpu.VMEM)
    sm = pl.BlockSpec(memory_space=pltpu.SMEM)
    hb = pl.BlockSpec(memory_space=pl.ANY)
    hbm = pl.BlockSpec(memory_space=pltpu.HBM)
    shard_rows = width // fsdp
    group = min(GROUP, cells)
    far = cells // group
    near = min(2, group)
    stride = group // near
    band, piece = 128 // near, 128 // group
    factor = 1.0 / (cells * fsdp)
    dma = pltpu.SemaphoreType.DMA
    outs = (((rows_n, width), BF), ((rows_n, width), F32), ((128, 6 * width), BF), ((16, 128), F32))
    far_n = max(far - 1, 1)
    LB = 256
    scratch = [
        ((rows_n, width), BF), ((rows_n, width), BF), ((1, rows_n), jnp.int32),
        ((width, 6 * width), BF), ((fsdp, 16, 128), F32), ((width, rows_n), BF), ((rows_n, rows_n), F32),
        ((4, rows_n, 128), BF), ((8, 128, rows_n), BF), ((4, rows_n, 128), BF), ((4, 128, rows_n), BF),
        ((4, rows_n, 128), BF), ((8, 80, rows_n), BF), ((8, rows_n, rows_n), BF),
        ((rows_n, width), BF), ((8, 64, rows_n), F32), ((8, 8, rows_n), F32), ((rows_n, 5 * width), BF),
        ((4, rows_n, 128), BF), ((8, 8, rows_n), F32), ((rows_n, rows_n), BF), ((rows_n, rows_n), BF),
        ((4, 128, rows_n), BF),
        ((rows_n, LB), F32), ((rows_n, LB), F32), ((8, LB), F32), ((8, LB), F32), ((rows_n, LB), BF), ((rows_n, LB), BF),
        ((16, width), F32),
        ((fsdp, 128, 6 * width), BF), ((2, 128, 6 * width), BF), ((2 * near - 1, band, 6 * width), BF),
        ((max(stride - 1, 1), piece, 6 * width), BF), ((far_n, piece, 6 * width), BF), ((128, 6 * width), BF),
        ((fsdp, 16, 128), F32), ((fsdp - 1, 16, 128), F32), ((16, 128), F32), ((group - 1, 16, 128), F32),
        ((16, 128), F32), ((far_n, 16, 128), F32),
    ]
    sems = [
        (18,), (4,), (5, 3), (5, 3), (3,), (3,), (8, 2), (8, 2), (8, 2 * near - 1), (8, 2 * near - 1), (8,), (8,),
        (8, far_n), (8, far_n), (8,), (8,), (3,), (3,), (group - 1,), (group - 1,), (far_n,), (far_n,),
    ]
    results = pl.pallas_call(
        functools.partial(layer_kernel, cells, fsdp, factor),
        out_shape=[jax.ShapeDtypeStruct(s, t) for s, t in outs],
        in_specs=[sm] + [hb] * 7 + [vm] * 2,
        out_specs=[hb] * 4,
        scratch_shapes=[pltpu.VMEM(s, t) for s, t in scratch] + [dma(s) for s in sems],
        compiler_params=pltpu.CompilerParams(
            vmem_limit_bytes=63 * 2**20 + 2**19, collective_id=0, has_side_effects=True
        ),
        name="layer",
    )(lengths, generate, *args)
    finals = (
        ((rows_n, width), BF), ((rows_n, width), F32), ((shard_rows, 3 * width), F32), ((shard_rows, width), F32),
        ((shard_rows, width), F32), ((shard_rows, width), F32), ((7, width // fsdp), F32), ((2, width // fsdp), F32),
    )
    buffers = list(outs) + list(finals[2:])
    return pl.pallas_call(
        finish_kernel,
        out_shape=[jax.ShapeDtypeStruct(s, t) for s, t in finals],
        in_specs=[hbm] * 4,
        out_specs=[hbm] * 8,
        scratch_shapes=[pltpu.VMEM(s, t) for s, t in buffers] + [dma((24,))],
        compiler_params=pltpu.CompilerParams(vmem_limit_bytes=63 * 2**20),
        name="finish",
    )(*results)


def body(cells, fsdp, tokens, cotangent, lengths, generate, *weights):
    _, rows_n, width = tokens.shape
    mixed, tokens_grad, *grads = call_layer(
        cells, fsdp, rows_n, width, lengths, generate, tokens[0], cotangent[0], *weights
    )
    return (mixed[None], tokens_grad[None], *grads)


def solution(mesh):
    split = P(("cells", "fsdp"), None, None)
    rows, cols = P("fsdp", None), P(None, "fsdp")
    return jax.shard_map(
        functools.partial(body, mesh.shape["cells"], mesh.shape["fsdp"]),
        mesh=mesh,
        in_specs=(split, split, P(("cells", "fsdp")), P(("cells", "fsdp"), None), rows, rows, rows, rows, cols, cols),
        out_specs=(split, split, rows, rows, rows, rows, cols, cols),
        check_vma=False,
    )
```

```python
import functools

import jax
import jax.numpy as jnp
from jax import lax
from jax.experimental import pallas as pl
from jax.experimental.pallas import tpu as pltpu
from jax.sharding import PartitionSpec as P

F32, BF = jnp.float32, jnp.bfloat16
MESH = pl.DeviceIdType.MESH
HEADS = 8
EPS = 1e-5
CHUNK = 384
GROUP = 8


def dot(a, b):
    return jnp.dot(a, b, preferred_element_type=F32)


def dot_t(a, b):
    return lax.dot_general(a, b, (((1,), (1,)), ((), ())), preferred_element_type=F32)


def col_sum(v):
    return jnp.sum(v, axis=0, keepdims=True)


def norm(v):
    centred = v - jnp.mean(v, axis=1, keepdims=True)
    r = lax.rsqrt(jnp.mean(centred * centred, axis=1, keepdims=True) + EPS)
    return centred * r, r


def norm_back(g, xhat, r):
    g_mean = jnp.mean(g, axis=1, keepdims=True)
    x_mean = jnp.mean(g * xhat, axis=1, keepdims=True)
    return r * (g - g_mean - xhat * x_mean)


def aligned(value, step):
    return pl.multiple_of(value, step)


def layer_kernel(
    cells, fsdp, factor,
    len_ref, gen_in, tok_in, cot_in, wq_in, wo_in, w1_in, w2_in, bias_in, gain_in,
    mixed_out, tgrad_out, sums_out, vec_out,
    X, COT, GEN, W, VEC, XT, VC, qp, QTz, KN, KT, VN, VT1, e, att, OT, rL, A5, dAn, dl, Z0, Z1, dQT,
    S, MX, eb0, eb1, vecg,
    G, R1, R2, R3, R3b, R4, R5, R6, V0, VR1, V1, VR2, V2, VR3,
    in_sem, out_sem, gs_sem, gr_sem, vs_sem, vr_sem,
    s1s, s1r, s2s, s2r, s3s, s3r, s3bs, s3br, s4s, s4r, s5s, s5r, s6s, s6r, v1s, v1r, v2s, v2r, v3s, v3r,
):
    rows_n, width = X.shape
    pairs = HEADS // 2
    RB = 512
    LB = 256
    cell = lax.axis_index("cells")
    shard = lax.axis_index("fsdp")
    group = min(GROUP, cells)
    far = cells // group
    low = lax.rem(cell, group)
    high = lax.div(cell, group)
    act, gf, nl, gb, gbr = (A5.at[:, pl.ds(i * width, width)] for i in range(5))
    dATz, mixed, tgrad = QTz, COT, S.at[:, pl.ds(0, width)]

    def near_shard(s):
        return s + 1 - 2 * lax.rem(s, 2)

    def far_shard(s):
        return s + 2 - 4 * lax.rem(lax.div(s, 2), 2)

    def fsdp_dev(s):
        return (cell, s)

    def low_dev(r):
        return (high * group + lax.rem(low + r, group), shard)

    def high_dev(r):
        return (lax.rem(high + r, far) * group + low, shard)

    s_near, s_far = near_shard(shard), far_shard(shard)
    s_diag = near_shard(s_far)
    others = (s_near, s_far, s_diag)

    def remote(src, dst, send, recv, device):
        return pltpu.make_async_remote_copy(
            src_ref=src, dst_ref=dst, send_sem=send, recv_sem=recv, device_id=device, device_id_type=MESH
        )

    barrier = pltpu.get_barrier_semaphore()
    for s in others:
        pl.semaphore_signal(barrier, inc=1, device_id=fsdp_dev(s), device_id_type=MESH)
    for r in range(1, group):
        pl.semaphore_signal(barrier, inc=1, device_id=low_dev(r), device_id_type=MESH)
    for r in range(1, group):
        pl.semaphore_signal(barrier, inc=1, device_id=(low_dev(r)[0], s_far), device_id_type=MESH)
    for r in range(1, far):
        pl.semaphore_signal(barrier, inc=1, device_id=high_dev(r), device_id_type=MESH)

    own = pl.ds(aligned(shard * 128, 128), 128)
    loads = []
    for p in range(pairs):
        for t in range(3):
            loads.append((wq_in.at[:, pl.ds(t * width + p * 128, 128)], W.at[own, pl.ds(p * CHUNK + t * 128, 128)]))
    for i, ref in enumerate((wo_in, w1_in, w2_in)):
        loads.append((ref, W.at[own, pl.ds((3 + i) * width, width)]))
    loads += [(tok_in, X), (gen_in, GEN), (cot_in, COT)]
    loads = [pltpu.make_async_copy(a, b, in_sem.at[i]) for i, (a, b) in enumerate(loads)]
    for copy in loads:
        copy.start()
    VEC[shard] = jnp.zeros((16, 128), F32)
    VEC[shard, 0:7, :] = bias_in[...].astype(F32)
    VEC[shard, 8:10, :] = gain_in[...].astype(F32)

    def w_copy(c, owner, hop, device):
        whole = isinstance(c, int) and c == pairs
        cols = pl.ds(3 * width, 3 * width) if whole else pl.ds(aligned(c * CHUNK, 128), CHUNK)
        part = W.at[pl.ds(aligned(owner * 128, 128), 128), cols]
        return remote(part, part, gs_sem.at[c, hop], gr_sem.at[c, hop], device)

    def vec_copy(i, s):
        return remote(VEC.at[shard], VEC.at[shard], vs_sem.at[i], vr_sem.at[i], fsdp_dev(s))

    parts = pairs + 1

    def w_send(c):
        w_copy(c, shard, 1, fsdp_dev(s_far)).start()
        w_copy(c, shard, 0, fsdp_dev(s_near)).start()

    def w_forward(c):
        w_copy(c, shard, 1, fsdp_dev(s_far)).wait_recv()
        w_copy(c, s_far, 2, fsdp_dev(s_near)).start()

    def w_ready(c):
        w_copy(c, shard, 0, fsdp_dev(s_near)).wait_recv()
        w_copy(c, s_far, 2, fsdp_dev(s_near)).wait_recv()

    for t in range(3):
        loads[t].wait()
    pl.semaphore_wait(barrier, fsdp - 1 + 2 * (group - 1) + far - 1)
    w_send(0)
    for i, s in enumerate(others):
        vec_copy(i, s).start()
    for t in range(3, 6):
        loads[t].wait()
    w_send(1)

    length = len_ref[0]
    loads[3 * pairs + 3].wait()
    loads[3 * pairs + 4].wait()
    XT[...] = X[...].T
    col_ids = lax.broadcasted_iota(jnp.int32, (1, rows_n), 1)
    visible = jnp.where((col_ids < length) & (GEN[...] == 0), 0.0, -1e9).astype(F32)
    VC[...] = jnp.broadcast_to(visible, (128, rows_n)).T
    QTz[...] = jnp.zeros_like(QTz)
    VT1[...] = jnp.ones_like(VT1)
    for t in range(6, 15):
        loads[t].wait()
    w_forward(0)
    w_send(2)
    w_send(3)
    for i, s in enumerate(others):
        vec_copy(i, s).wait_recv()
    w_ready(0)

    def bias_row(i):
        return jnp.concatenate([VEC[s, i : i + 1, :] for s in range(fsdp)], 1)

    def project(p, part):
        base = p * CHUNK
        if part == 0:
            pr = dot(X[...], W[:, pl.ds(aligned(base, 128), 256)])
            q = (pr[:, :128] + VEC[p, 0:1, :]).astype(BF) * jnp.asarray(0.125, BF)
            qp[p] = q
            KN[p] = pr[:, 128:256].astype(BF)
        if part == 1:
            pr = dot(X[...], W[:, pl.ds(aligned(base + 256, 128), 128)])
            VN[p] = (pr + VEC[p, 1:2, :]).astype(BF)
            qt = qp[p].T
            QTz[2 * p, 0:64, :] = qt[0:64]
            QTz[2 * p + 1, 64:128, :] = qt[64:128]
        if part == 2:
            KT[p] = KN[p].T
            vt = VN[p].T
            VT1[2 * p, 0:64, :] = vt[0:64]
            VT1[2 * p + 1, 0:64, :] = vt[64:128]

    units = HEADS * (rows_n // LB)
    per_head = rows_n // LB
    per_pair = 2 * per_head

    def unit(u):
        return u // per_head, u // per_pair, pl.ds(aligned((u % per_head) * LB, LB), LB)

    def score(u, n):
        h, p, _ = unit(jnp.minimum(u, units - 1))
        b = n % per_head
        raw = dot(KN[p], QTz[h, :, LB * b : LB * b + LB])
        for r in range(per_head):
            rows = slice(LB * r, LB * r + LB)
            w = VC[rows, :]
            part = raw[rows] + jnp.concatenate([w, w], 1)
            if r == b:
                keys = lax.broadcasted_iota(jnp.int32, (LB, LB), 0)
                part = jnp.where(keys == lax.broadcasted_iota(jnp.int32, (LB, LB), 1), raw[rows], part)
            S[rows, LB * (n % 4) : LB * (n % 4) + LB] = part

    def peak(n):
        MX[n % 4, 0:1, :] = jnp.max(S[:, LB * (n % 4) : LB * (n % 4) + LB], axis=0, keepdims=True)

    def weigh(u, n):
        h, p, _ = unit(u)
        b = n % per_head
        v = jnp.exp(S[:, LB * (n % 4) : LB * (n % 4) + LB] - MX[n % 4, 0:1, :]).astype(BF)
        e[h, :, LB * b : LB * b + LB] = v
        slots[n % 2][...] = v

    def mix(u, n):
        h, p, cols = unit(jnp.maximum(u, 0))
        o = dot(VT1[h], slots[n % 2][...])
        r = 1.0 / o[64:65, :]
        rL[h, 0:1, cols] = r
        OT[h, :, cols] = o[0:64, :] * r

    slots = (eb0, eb1)
    for i in range(3):
        project(0, i)
    w_send(pairs)
    score(0, 0)
    score(1, 1)
    peak(0)

    def forward_pair(p, is_last):
        w_forward(pairs if is_last else p + 1)
        for n in range(per_pair):
            if n == 3 and not is_last:
                w_ready(p + 1)
            if not is_last and 3 <= n < 6:
                project(p + 1, n - 3)
            u = per_pair * p + n
            score(u + 2, n + 2)
            weigh(u, n)
            peak(n + 1)
            mix(u - 1, n - 1)
        return 0

    lax.fori_loop(0, pairs - 1, lambda p, _: forward_pair(p, False), 0)
    forward_pair(pairs - 1, True)
    mix(units - 1, per_pair - 1)
    for p in range(pairs):
        ot = jnp.concatenate([OT[2 * p], OT[2 * p + 1]], 0).astype(BF)
        att[:, 128 * p : 128 * p + 128] = ot.T
    w_ready(pairs)
    loads[3 * pairs + 5].wait()

    wo, w1, w2 = (pl.ds((3 + i) * width, width) for i in range(3))
    vecg[...] = jnp.zeros_like(vecg)

    def rows_step(i, _):
        r0 = aligned(i * RB, RB)
        rows = pl.ds(r0, RB)
        gain0, gain1 = bias_row(8), bias_row(9)
        summed = X[rows, :].astype(F32) + dot(att[rows, :], W[:, wo]) + bias_row(2)
        xh1, rs1 = norm(summed)
        normed = xh1 * gain0 + bias_row(5)
        n_low = normed.astype(BF)
        before = dot(n_low, W[:, w1]) + bias_row(3)
        cdf = 0.5 * (1.0 + lax.erf(before * (2.0**-0.5)))
        pdf = jnp.exp(-0.5 * before * before) * (2.0 * jnp.pi) ** -0.5
        a_low = (before * cdf).astype(BF)
        slope = cdf + before * pdf
        second = normed + dot(a_low, W[:, w2]) + bias_row(4)
        xh2, rs2 = norm(second)
        valid = (lax.broadcasted_iota(jnp.int32, (RB, 1), 0) + r0 < length).astype(F32)
        g = COT[rows, :].astype(F32) * valid
        mixed[rows, :] = ((xh2 * gain1 + bias_row(6)) * valid).astype(BF)
        g_second = norm_back(g * gain1, xh2, rs2)
        g_feed = g_second.astype(BF)
        g_before = (slope * dot_t(g_feed, W[:, w2])).astype(BF)
        g_normed = g_second + dot_t(g_before, W[:, w1])
        g_summed = norm_back(g_normed * gain0, xh1, rs1)
        g_branch = g_summed.astype(BF)
        g_att = dot_t(g_branch, W[:, wo]).astype(BF)
        act[rows, :] = a_low
        gf[rows, :] = g_feed
        nl[rows, :] = n_low
        gb[rows, :] = g_before
        gbr[rows, :] = g_branch
        tgrad[rows, :] = g_summed
        vecg[2:3, :] += col_sum(g_branch.astype(F32))
        vecg[3:4, :] += col_sum(g_before.astype(F32))
        vecg[4:5, :] += col_sum(g_feed.astype(F32))
        vecg[5:6, :] += col_sum(g_normed)
        vecg[6:7, :] += col_sum(g)
        vecg[8:9, :] += col_sum(g_normed * xh1)
        vecg[9:10, :] += col_sum(g * xh2)
        for p in range(pairs):
            dAn[p, rows, :] = g_att[:, 128 * p : 128 * p + 128]
        return 0

    lax.fori_loop(0, rows_n // RB, rows_step, 0)
    mixed_copy = pltpu.make_async_copy(mixed, mixed_out, out_sem.at[0])
    mixed_copy.start()

    near, stride = min(2, group), max(group // 2, 1)
    side, place = lax.rem(low, near), lax.div(low, near)
    band = 128 // near
    piece = band // stride
    own_rows = pl.ds(aligned(side * band + place * piece, piece), piece)

    def cell_dev(side_to, place_to, s):
        return (high * group + lax.rem(place_to, stride) * near + side_to, s)

    def cols_of(c):
        if isinstance(c, tuple):
            return 4 + c[0], pl.ds(aligned(4 * width + c[0] * 256, 256), 256)
        return c, pl.ds(c * width, width)

    def s1_all(c):
        i, cols = cols_of(c)
        return [
            remote(G.at[s, :, cols], R1.at[k, :, cols], s1s.at[i, k], s1r.at[i, k], fsdp_dev(s_near))
            for k, s in enumerate((s_near, s_diag))
        ]

    def s1_start(c):
        for copy in s1_all(c):
            copy.start()

    def s2_all(c):
        i, cols = cols_of(c)
        mine = pl.ds(aligned(side * band, band), band)
        other = pl.ds(aligned((near - 1 - side) * band, band), band)
        to = near - 1 - side
        plan = [(s_far, mine, side, s_far)]
        if near > 1:
            plan += [(shard, other, to, shard), (s_far, other, to, s_far)]
        return [
            remote(G.at[s, rows, cols], R2.at[k, :, cols], s2s.at[i, k], s2r.at[i, k], cell_dev(to_side, place, s))
            for k, (s, rows, to_side, _) in enumerate(plan)
        ]

    def s2_start(c):
        pair_sum(c)
        for copy in s2_all(c):
            copy.start()

    def s3_one(c, r):
        i, cols = cols_of(c)
        to = lax.rem(place + r, stride)
        rows = pl.ds(aligned(side * band + to * piece, piece), piece)
        return remote(
            G.at[shard, rows, cols], R3.at[pl.ds((r - 1) * piece, piece), cols], s3s.at[i], s3r.at[i],
            cell_dev(side, place + r, shard),
        )

    def s3_whole(c):
        i, cols = cols_of(c)
        part = R3.at[:, cols]
        return remote(part, part, s3s.at[i], s3r.at[i], cell_dev(side, place + 1, shard))

    def band_sum(c):
        i, cols = cols_of(c)
        mine = pl.ds(aligned(side * band, band), band)
        total = G[shard, mine, cols].astype(F32)
        for k, copy in enumerate(s2_all(c)):
            copy.wait_recv()
            total = total + R2[k, :, cols].astype(F32)
        G[shard, mine, cols] = total.astype(BF)

    def s3_start(c):
        band_sum(c)
        for r in range(1, stride):
            s3_one(c, r).start()

    odd = lax.rem(place, 2)
    beside = place + 1 - 2 * odd
    half = 2 * piece
    half_rows = pl.ds(aligned(side * band + odd * half, half), half)

    def h3_copy(c):
        i, cols = cols_of(c)
        rows = pl.ds(aligned(side * band + (1 - odd) * half, half), half)
        return remote(
            G.at[shard, rows, cols], R3.at[pl.ds(0, half), cols], s3s.at[i], s3r.at[i], cell_dev(side, beside, shard)
        )

    def h3_start(c):
        band_sum(c)
        h3_copy(c).start()

    def h4_copy(c):
        i, cols = cols_of(c)
        return remote(
            G.at[shard, half_rows, cols], R5.at[:, cols], s5s.at[i], s5r.at[i], cell_dev(side, place + 2, shard)
        )

    def h4_start(c):
        i, cols = cols_of(c)
        h3_copy(c).wait_recv()
        G[shard, half_rows, cols] = (
            G[shard, half_rows, cols].astype(F32) + R3[0:half, cols].astype(F32)
        ).astype(BF)
        h4_copy(c).start()

    def h5_all(c):
        i, cols = cols_of(c)
        part = R4.at[half_rows, cols]
        to = near - 1 - side
        return [
            remote(part, part, s4s.at[i], s4r.at[i], cell_dev(a, b, shard))
            for a, b in ((side, beside), (to, place), (to, beside))
        ]

    def h5_whole(c):
        i, cols = cols_of(c)
        part = R4.at[pl.ds(0, 3 * half), cols]
        return remote(part, part, s4s.at[i], s4r.at[i], cell_dev(side, beside, shard))

    def h5_start(c):
        i, cols = cols_of(c)
        h4_copy(c).wait_recv()
        total = G[shard, half_rows, cols].astype(F32) + R5[:, cols].astype(F32)
        R4[half_rows, cols] = total.astype(BF)
        if far > 1:
            for r in range(1, far):
                far_one(c, r, half_rows, half).start()
            for r in range(1, far):
                far_one(c, r, half_rows, half).wait_recv()
                total = total + far_slot(c, r, half)[...].astype(F32)
            for r in range(1, far):
                far_one(c, r, half_rows, half).wait_send()
            R4[half_rows, cols] = total.astype(BF)
        for copy in h5_all(c):
            copy.start()

    def far_slot(c, r, count):
        i, cols = cols_of(c)
        return R3b.at[r - 1, pl.ds(0, count), pl.ds((i % 2) * width, 256 if isinstance(c, tuple) else width)]

    def far_one(c, r, rows, count):
        i, cols = cols_of(c)
        return remote(
            R4.at[rows, cols], far_slot(c, r, count), s3bs.at[i, r - 1], s3br.at[i, r - 1], high_dev(r)
        )

    def s4_one(c, r):
        i, cols = cols_of(c)
        part = R4.at[own_rows, cols]
        return remote(part, part, s4s.at[i], s4r.at[i], low_dev(r))

    def s4_whole(c):
        i, cols = cols_of(c)
        part = R4.at[pl.ds(0, 128 - piece), cols]
        return remote(part, part, s4s.at[i], s4r.at[i], low_dev(1))

    def s4_start(c):
        i, cols = cols_of(c)
        total = G[shard, own_rows, cols].astype(F32)
        s3_whole(c).wait_recv()
        for r in range(1, stride):
            total = total + R3[(r - 1) * piece : r * piece, cols].astype(F32)
        share(c, total)

    def share(c, total):
        i, cols = cols_of(c)
        R4[own_rows, cols] = total.astype(BF)
        if far > 1:
            for r in range(1, far):
                far_one(c, r, own_rows, piece).start()
            for r in range(1, far):
                far_one(c, r, own_rows, piece).wait_recv()
                total = total + far_slot(c, r, piece)[...].astype(F32)
            for r in range(1, far):
                far_one(c, r, own_rows, piece).wait_send()
            R4[own_rows, cols] = total.astype(BF)
        for r in range(1, group):
            s4_one(c, r).start()

    def d_one(c, k, s):
        i, cols = cols_of(c)
        to = lax.rem(low + k, group)
        rows = pl.ds(aligned(lax.rem(to, near) * band + lax.div(to, near) * piece, piece), piece)
        slot = k - 1 if s is shard else group - 1 + k
        return remote(G.at[s, rows, cols], R6.at[slot], s6s.at[0], s6r.at[0], (high * group + to, s))

    def d_all(c):
        return [d_one(c, k, s_far) for k in range(group)] + [d_one(c, k, shard) for k in range(1, group)]

    def d_whole(c):
        return remote(R6, R6, s6s.at[0], s6r.at[0], low_dev(1))

    def pair_sum(c):
        i, cols = cols_of(c)
        for copy in s1_all(c):
            copy.wait_recv()
        G[s_far, :, cols] = (G[s_far, :, cols].astype(F32) + R1[1, :, cols].astype(F32)).astype(BF)
        G[shard, :, cols] = (G[shard, :, cols].astype(F32) + R1[0, :, cols].astype(F32)).astype(BF)

    def d_start(c):
        pair_sum(c)
        for copy in d_all(c):
            copy.start()

    def d4_start(c):
        i, cols = cols_of(c)
        total = G[shard, own_rows, cols].astype(F32)
        d_whole(c).wait_recv()
        for k in range(2 * group - 1):
            total = total + R6[k].astype(F32)
        share(c, total)

    halved = [0, 1, 2, 3, (0,), (1,)]
    direct = [(2,), (3,)]

    def drain():
        for c in halved + direct:
            for copy in s1_all(c):
                copy.wait_send()
        for c in halved + direct[:1]:
            for copy in s2_all(c):
                copy.wait_send()
        for c in halved:
            h3_copy(c).wait_send()
            h4_copy(c).wait_send()
            h5_whole(c).wait_send()
        s3_whole(direct[0]).wait_send()
        d_whole(direct[1]).wait_send()
        for c in direct:
            s4_whole(c).wait_send()

    for i, (left, right) in enumerate(((att, gbr), (nl, gb), (act, gf))):
        term = (dot(left[...].T, right[...]) * factor).astype(BF)
        for s in range(fsdp):
            G[s, :, width * i : width * i + width] = term[128 * s : 128 * s + 128, :]
        s1_start(i)
    s2_start(0)

    def prepare(p, _):
        gt = dAn[p].T.astype(F32)
        parts = []
        for hh in range(2):
            h = 2 * p + hh
            x = (gt[64 * hh : 64 * hh + 64, :] * rL[h, 0:1, :]).astype(BF)
            dl[h, 0:1, :] = col_sum(x.astype(F32) * OT[h])
            dATz[h, 64 * hh : 64 * hh + 64, :] = x
            parts.append(x)
        dAn[p] = jnp.concatenate(parts, 0).T
        return 0

    lax.fori_loop(0, pairs, prepare, 0)
    s2_start(1)
    s2_start(2)

    def score_grads(p, hh, n, z_ref):
        cols = pl.ds(n * LB, LB)
        h = 2 * p + hh
        shifted = dot(VN[p], dATz[h, :, cols]) - dl[h, 0:1, cols]
        z_ref[:, cols] = (shifted * e[h, :, cols].astype(F32)).astype(BF)

    def query_grads(p, hh, n, z_ref):
        cols = pl.ds(n * LB, LB)
        half = slice(64 * hh, 64 * hh + 64)
        dQT[lax.rem(p, 2), half, cols] = (dot(KT[p, half, :], z_ref[:, cols]) * 0.125).astype(BF)

    first = lax.broadcasted_iota(jnp.int32, (LB, 128), 1) < 64
    dka = S.at[:, pl.ds(width, 128)]

    def value_grads(p, _):
        cols = pl.ds(aligned(p * CHUNK + 256, 128), 128)
        for n in range(per_head):
            rows = pl.ds(n * LB, LB)
            dv0 = dot(e[2 * p, rows, :], dAn[p])
            dv1 = dot(e[2 * p + 1, rows, :], dAn[p])
            A5[rows, cols] = jnp.where(first, dv0, dv1).astype(BF)
        return 0

    def key_grads(p, hh, n, z_ref):
        rows = pl.ds(n * LB, LB)
        dk = dot(z_ref[rows, :], qp[p])
        if hh == 0:
            dka[rows, :] = dk
        else:
            c = aligned(p * CHUNK, 128)
            A5[rows, pl.ds(c + 128, 128)] = jnp.where(first, dka[rows, :], dk).astype(BF)

    def put_terms(first_col, source):
        term = (dot(XT[...], source) * factor).astype(BF)
        for n in range(fsdp):
            G[n, :, pl.ds(first_col, source.shape[1])] = term[128 * n : 128 * n + 128, :]

    def pair_term(p):
        put_terms(aligned(4 * width + p * 256, 256), A5[:, pl.ds(aligned(p * CHUNK, 128), 256)])

    def pair_end(p):
        c = aligned(p * CHUNK, 128)
        A5[:, pl.ds(c, 128)] = dQT[lax.rem(p, 2)].T
        vecg[0:1, pl.ds(aligned(p * 128, 128), 128)] = col_sum(A5[:, pl.ds(c, 128)].astype(F32))

    lax.fori_loop(0, pairs, value_grads, 0)
    h3_start(0)
    all_dv = jnp.concatenate([A5[:, CHUNK * p + 256 : CHUNK * p + 384] for p in range(pairs)], 1)
    put_terms(3 * width, all_dv)
    s1_start(3)
    vecg[1:2, :] = col_sum(all_dv.astype(F32))

    def backward_pair(p, _):
        before = jnp.maximum(p - 1, 0)
        for n in range(per_head):
            key_grads(before, 1, n, Z1)
            if n == 0:
                query_grads(before, 1, per_head - 1, Z1)
            else:
                query_grads(p, 0, n - 1, Z0)
            score_grads(p, 0, n, Z0)
        pair_end(before)
        pl.when(p == 0)(lambda: s2_start(3))
        pl.when(p == 1)(lambda: h3_start(2))
        pl.when(p >= 2)(lambda: s2_start((p - 2,)))
        pl.when(p == 2)(lambda: h3_start(3))
        pl.when(p == 2)(lambda: h4_start(2))
        pl.when(p == 3)(lambda: h3_start((0,)))
        pl.when(p == 3)(lambda: h4_start(3))
        pl.when(p == 3)(lambda: h5_start(2))
        for n in range(per_head):
            key_grads(p, 0, n, Z0)
            if n == 0:
                query_grads(p, 0, per_head - 1, Z0)
            else:
                query_grads(p, 1, n - 1, Z1)
            score_grads(p, 1, n, Z1)
            if n == 0:
                pair_term(before)
            if n == 2:
                pl.when(p >= 1)(lambda: s1_start((p - 1,)))
        pl.when(p == 0)(lambda: h3_start(1))
        pl.when(p == 0)(lambda: h4_start(0))
        pl.when(p == 1)(lambda: h4_start(1))
        pl.when(p == 1)(lambda: h5_start(0))
        pl.when(p == 2)(lambda: h5_start(1))
        return 0

    lax.fori_loop(0, pairs, backward_pair, 0)
    last = pairs - 1
    s2_start((2,))
    for n in range(per_head):
        key_grads(last, 1, n, Z1)
    query_grads(last, 1, per_head - 1, Z1)
    pair_end(last)
    pair_term(last)
    s1_start((3,))

    for s in range(fsdp):
        V0[s] = vecg[:, 128 * s : 128 * s + 128] * factor

    def v1_copy(i, s):
        return remote(V0.at[s], VR1.at[i], v1s.at[i], v1r.at[i], fsdp_dev(s))

    def v2_copy(r):
        return remote(V1, VR2.at[r - 1], v2s.at[r - 1], v2r.at[r - 1], low_dev(r))

    def v3_copy(r):
        return remote(V2, VR3.at[r - 1], v3s.at[r - 1], v3r.at[r - 1], high_dev(r))

    for i, s in enumerate(others):
        v1_copy(i, s).start()
    h5_start(3)
    h3_start((1,))
    h4_start((0,))

    def tokens_step(i, _):
        rows = pl.ds(aligned(i * 256, 256), 256)
        tgrad[rows, :] += dot_t(A5[rows, 0 : 3 * width], W[:, 0 : 3 * width])
        return 0

    steps = rows_n // 256
    tokens_step(0, 0)
    d_start((3,))
    lax.fori_loop(1, steps // 2 + 1, tokens_step, 0)
    h4_start((1,))
    h5_start((0,))
    lax.fori_loop(steps // 2 + 1, steps, tokens_step, 0)
    tgrad_copy = pltpu.make_async_copy(tgrad, tgrad_out, out_sem.at[1])
    tgrad_copy.start()
    for i, s in enumerate(others):
        v1_copy(i, s).wait_recv()
    V1[...] = V0[shard] + VR1[0] + VR1[1] + VR1[2]
    for r in range(1, group):
        v2_copy(r).start()
    s3_start((2,))
    h5_start((1,))
    d4_start((3,))
    s4_start((2,))
    total = V1[...]
    for r in range(1, group):
        v2_copy(r).wait_recv()
        total = total + VR2[r - 1]
    if far > 1:
        V2[...] = total
        for r in range(1, far):
            v3_copy(r).start()
        for r in range(1, far):
            v3_copy(r).wait_recv()
            total = total + VR3[r - 1]
    VR1[0] = total
    vec_end = pltpu.make_async_copy(VR1.at[0], vec_out, out_sem.at[2])
    vec_end.start()
    for c in halved:
        h5_whole(c).wait_recv()
    early = 5 * width
    early_copy = pltpu.make_async_copy(R4.at[:, pl.ds(0, early)], sums_out.at[:, pl.ds(0, early)], out_sem.at[3])
    early_copy.start()
    for c in direct:
        s4_whole(c).wait_recv()
    late_cols = pl.ds(early, width)
    late_copy = pltpu.make_async_copy(R4.at[:, late_cols], sums_out.at[:, late_cols], out_sem.at[4])
    late_copy.start()

    for c in range(parts):
        w_copy(c, shard, 1, fsdp_dev(s_far)).wait_send()
        w_copy(c, shard, 0, fsdp_dev(s_near)).wait_send()
        w_copy(c, s_far, 2, fsdp_dev(s_near)).wait_send()

    drain()
    for i, s in enumerate(others):
        vec_copy(i, s).wait_send()
        v1_copy(i, s).wait_send()
    for r in range(1, group):
        v2_copy(r).wait_send()
    for r in range(1, far):
        v3_copy(r).wait_send()
    for copy in (mixed_copy, tgrad_copy, vec_end, early_copy, late_copy):
        copy.wait()


def finish_kernel(
    mixed_in, tgrad_in, sums_in, vec_in, mixed_out, tgrad_out, qkv_out, wo_out, w1_out, w2_out, bias_out, gain_out,
    M, T, R, V, Q, O, A, B, bias, gain, sem,
):
    width = M.shape[1]
    pairs = HEADS // 2
    steps = 4
    rows = M.shape[0] // steps
    ins, outs = [], []

    def start(src, dst):
        copy = pltpu.make_async_copy(src, dst, sem.at[len(ins) + len(outs)])
        copy.start()
        return copy

    for i in range(steps):
        part = pl.ds(i * rows, rows)
        ins.append(start(tgrad_in.at[part], T.at[part]))
        ins.append(start(mixed_in.at[part], M.at[part]))
    ins.append(start(sums_in, R))
    ins.append(start(vec_in, V))
    for i in range(steps):
        part = pl.ds(i * rows, rows)
        ins[2 * i].wait()
        outs.append(start(T.at[part], tgrad_out.at[part]))
        ins[2 * i + 1].wait()
        outs.append(start(M.at[part], mixed_out.at[part]))
    ins[2 * steps].wait()
    for p in range(pairs):
        for t in range(2):
            c = 4 * width + 256 * p + 128 * t
            Q[:, t * width + p * 128 : t * width + p * 128 + 128] = R[:, c : c + 128].astype(F32)
    Q[:, 2 * width :] = R[:, 3 * width : 4 * width].astype(F32)
    outs.append(start(Q, qkv_out))
    for i, ref in enumerate((O, A, B)):
        ref[...] = R[:, i * width : i * width + width].astype(F32)
    for src, dst in ((O, wo_out), (A, w1_out), (B, w2_out)):
        outs.append(start(src, dst))
    ins[2 * steps + 1].wait()
    bias[...] = V[0:7, :]
    gain[...] = V[8:10, :]
    outs.append(start(bias, bias_out))
    outs.append(start(gain, gain_out))
    for copy in outs:
        copy.wait()


def call_layer(cells, fsdp, rows_n, width, lengths, generate, *args):
    vm = pl.BlockSpec(memory_space=pltpu.VMEM)
    sm = pl.BlockSpec(memory_space=pltpu.SMEM)
    hb = pl.BlockSpec(memory_space=pl.ANY)
    hbm = pl.BlockSpec(memory_space=pltpu.HBM)
    shard_rows = width // fsdp
    group = min(GROUP, cells)
    far = cells // group
    near = min(2, group)
    stride = group // near
    band, piece = 128 // near, 128 // group
    factor = 1.0 / (cells * fsdp)
    dma = pltpu.SemaphoreType.DMA
    outs = (((rows_n, width), BF), ((rows_n, width), F32), ((128, 6 * width), BF), ((16, 128), F32))
    far_n = max(far - 1, 1)
    LB = 256
    scratch = [
        ((rows_n, width), BF), ((rows_n, width), BF), ((1, rows_n), jnp.int32),
        ((width, 6 * width), BF), ((fsdp, 16, 128), F32), ((width, rows_n), BF), ((rows_n, 128), F32),
        ((4, rows_n, 128), BF), ((8, 128, rows_n), BF), ((4, rows_n, 128), BF), ((4, 128, rows_n), BF),
        ((4, rows_n, 128), BF), ((8, 80, rows_n), BF), ((8, rows_n, rows_n), BF),
        ((rows_n, width), BF), ((8, 64, rows_n), F32), ((8, 8, rows_n), F32), ((rows_n, 5 * width), BF),
        ((4, rows_n, 128), BF), ((8, 8, rows_n), F32), ((rows_n, rows_n), BF), ((rows_n, rows_n), BF),
        ((2, 128, rows_n), BF),
        ((rows_n, 4 * LB), F32), ((4, 8, LB), F32), ((rows_n, LB), BF), ((rows_n, LB), BF),
        ((16, width), F32),
        ((fsdp, 128, 6 * width), BF), ((2, 128, 6 * width), BF), ((2 * near - 1, band, 6 * width), BF),
        (((stride - 1) * piece, 6 * width), BF), ((far_n, 2 * piece, 2 * width), BF), ((128, 6 * width), BF),
        ((2 * piece, 6 * width), BF), ((2 * group - 1, piece, 256), BF),
        ((fsdp, 16, 128), F32), ((fsdp - 1, 16, 128), F32), ((16, 128), F32), ((group - 1, 16, 128), F32),
        ((16, 128), F32), ((far_n, 16, 128), F32),
    ]
    sems = [
        (18,), (5,), (5, 3), (5, 3), (3,), (3,), (8, 2), (8, 2), (8, 2 * near - 1), (8, 2 * near - 1), (8,), (8,),
        (8, far_n), (8, far_n), (8,), (8,), (8,), (8,), (1,), (1,), (3,), (3,), (group - 1,), (group - 1,), (far_n,), (far_n,),
    ]
    results = pl.pallas_call(
        functools.partial(layer_kernel, cells, fsdp, factor),
        out_shape=[jax.ShapeDtypeStruct(s, t) for s, t in outs],
        in_specs=[sm] + [hb] * 7 + [vm] * 2,
        out_specs=[hb] * 4,
        scratch_shapes=[pltpu.VMEM(s, t) for s, t in scratch] + [dma(s) for s in sems],
        compiler_params=pltpu.CompilerParams(
            vmem_limit_bytes=63 * 2**20 + 2**19, collective_id=0, has_side_effects=True
        ),
        name="layer",
    )(lengths, generate, *args)
    finals = (
        ((rows_n, width), BF), ((rows_n, width), F32), ((shard_rows, 3 * width), F32), ((shard_rows, width), F32),
        ((shard_rows, width), F32), ((shard_rows, width), F32), ((7, width // fsdp), F32), ((2, width // fsdp), F32),
    )
    buffers = list(outs) + list(finals[2:])
    return pl.pallas_call(
        finish_kernel,
        out_shape=[jax.ShapeDtypeStruct(s, t) for s, t in finals],
        in_specs=[hbm] * 4,
        out_specs=[hbm] * 8,
        scratch_shapes=[pltpu.VMEM(s, t) for s, t in buffers] + [dma((24,))],
        compiler_params=pltpu.CompilerParams(vmem_limit_bytes=63 * 2**20),
        name="finish",
    )(*results)


def body(cells, fsdp, tokens, cotangent, lengths, generate, *weights):
    _, rows_n, width = tokens.shape
    mixed, tokens_grad, *grads = call_layer(
        cells, fsdp, rows_n, width, lengths, generate, tokens[0], cotangent[0], *weights
    )
    return (mixed[None], tokens_grad[None], *grads)


def solution(mesh):
    split = P(("cells", "fsdp"), None, None)
    rows, cols = P("fsdp", None), P(None, "fsdp")
    return jax.shard_map(
        functools.partial(body, mesh.shape["cells"], mesh.shape["fsdp"]),
        mesh=mesh,
        in_specs=(split, split, P(("cells", "fsdp")), P(("cells", "fsdp"), None), rows, rows, rows, rows, cols, cols),
        out_specs=(split, split, rows, rows, rows, rows, cols, cols),
        check_vma=False,
    )
```

```python
import functools

import jax
import jax.numpy as jnp
from jax import lax
from jax.experimental import pallas as pl
from jax.experimental.pallas import tpu as pltpu
from jax.sharding import PartitionSpec as P

F32, BF = jnp.float32, jnp.bfloat16
MESH = pl.DeviceIdType.MESH
HEADS = 8
EPS = 1e-5
CHUNK = 384
GROUP = 8


def dot(a, b):
    return jnp.dot(a, b, preferred_element_type=F32)


def dot_t(a, b):
    return lax.dot_general(a, b, (((1,), (1,)), ((), ())), preferred_element_type=F32)


def col_sum(v):
    return jnp.sum(v, axis=0, keepdims=True)


def norm(v):
    centred = v - jnp.mean(v, axis=1, keepdims=True)
    r = lax.rsqrt(jnp.mean(centred * centred, axis=1, keepdims=True) + EPS)
    return centred * r, r


def norm_back(g, xhat, r):
    g_mean = jnp.mean(g, axis=1, keepdims=True)
    x_mean = jnp.mean(g * xhat, axis=1, keepdims=True)
    return r * (g - g_mean - xhat * x_mean)


def aligned(value, step):
    return pl.multiple_of(value, step)


def layer_kernel(
    cells, fsdp, factor,
    len_ref, gen_in, tok_in, cot_in, wq_in, wo_in, w1_in, w2_in, bias_in, gain_in,
    mixed_out, tgrad_out, sums_out, vec_out,
    X, COT, GEN, W, VEC, XT, VC, qp, QTz, KN, KT, VN, VT1, e, att, OT, rL, A5, dAn, dl, Z0, Z1, dQT,
    S, MX, eb0, eb1, vecg,
    G, R1, R2, R3, R3b, R4, R5, R6, V0, VR1, V1, VR2, V2, VR3,
    in_sem, out_sem, gs_sem, gr_sem, vs_sem, vr_sem,
    s1s, s1r, s2s, s2r, s3s, s3r, s3bs, s3br, s4s, s4r, s5s, s5r, s6s, s6r, v1s, v1r, v2s, v2r, v3s, v3r,
):
    rows_n, width = X.shape
    pairs = HEADS // 2
    RB = 512
    LB = 256
    cell = lax.axis_index("cells")
    shard = lax.axis_index("fsdp")
    group = min(GROUP, cells)
    far = cells // group
    low = lax.rem(cell, group)
    high = lax.div(cell, group)
    act, gf, nl, gb, gbr = (A5.at[:, pl.ds(i * width, width)] for i in range(5))
    dATz, mixed, tgrad = QTz, COT, S.at[:, pl.ds(0, width)]

    def near_shard(s):
        return s + 1 - 2 * lax.rem(s, 2)

    def far_shard(s):
        return s + 2 - 4 * lax.rem(lax.div(s, 2), 2)

    def fsdp_dev(s):
        return (cell, s)

    def low_dev(r):
        return (high * group + lax.rem(low + r, group), shard)

    def high_dev(r):
        return (lax.rem(high + r, far) * group + low, shard)

    s_near, s_far = near_shard(shard), far_shard(shard)
    s_diag = near_shard(s_far)
    others = (s_near, s_far, s_diag)

    def remote(src, dst, send, recv, device):
        return pltpu.make_async_remote_copy(
            src_ref=src, dst_ref=dst, send_sem=send, recv_sem=recv, device_id=device, device_id_type=MESH
        )

    barrier = pltpu.get_barrier_semaphore()
    for s in others:
        pl.semaphore_signal(barrier, inc=1, device_id=fsdp_dev(s), device_id_type=MESH)
    for r in range(1, group):
        pl.semaphore_signal(barrier, inc=1, device_id=low_dev(r), device_id_type=MESH)
    for r in range(1, group):
        pl.semaphore_signal(barrier, inc=1, device_id=(low_dev(r)[0], s_far), device_id_type=MESH)
    for r in range(1, far):
        pl.semaphore_signal(barrier, inc=1, device_id=high_dev(r), device_id_type=MESH)

    own = pl.ds(aligned(shard * 128, 128), 128)
    loads = []
    for p in range(pairs):
        for t in range(3):
            loads.append((wq_in.at[:, pl.ds(t * width + p * 128, 128)], W.at[own, pl.ds(p * CHUNK + t * 128, 128)]))
    for i, ref in enumerate((wo_in, w1_in, w2_in)):
        loads.append((ref, W.at[own, pl.ds((3 + i) * width, width)]))
    loads += [(tok_in, X), (gen_in, GEN), (cot_in, COT)]
    loads = [pltpu.make_async_copy(a, b, in_sem.at[i]) for i, (a, b) in enumerate(loads)]
    for copy in loads:
        copy.start()
    VEC[shard] = jnp.zeros((16, 128), F32)
    VEC[shard, 0:7, :] = bias_in[...].astype(F32)
    VEC[shard, 8:10, :] = gain_in[...].astype(F32)

    def w_copy(c, owner, hop, device):
        whole = isinstance(c, int) and c == pairs
        cols = pl.ds(3 * width, 3 * width) if whole else pl.ds(aligned(c * CHUNK, 128), CHUNK)
        part = W.at[pl.ds(aligned(owner * 128, 128), 128), cols]
        return remote(part, part, gs_sem.at[c, hop], gr_sem.at[c, hop], device)

    def vec_copy(i, s):
        return remote(VEC.at[shard], VEC.at[shard], vs_sem.at[i], vr_sem.at[i], fsdp_dev(s))

    parts = pairs + 1

    def w_send(c):
        w_copy(c, shard, 1, fsdp_dev(s_far)).start()
        w_copy(c, shard, 0, fsdp_dev(s_near)).start()

    def w_forward(c):
        w_copy(c, shard, 1, fsdp_dev(s_far)).wait_recv()
        w_copy(c, s_far, 2, fsdp_dev(s_near)).start()

    def w_ready(c):
        w_copy(c, shard, 0, fsdp_dev(s_near)).wait_recv()
        w_copy(c, s_far, 2, fsdp_dev(s_near)).wait_recv()

    for t in range(3):
        loads[t].wait()
    pl.semaphore_wait(barrier, fsdp - 1 + 2 * (group - 1) + far - 1)
    w_send(0)
    for i, s in enumerate(others):
        vec_copy(i, s).start()
    for t in range(3, 6):
        loads[t].wait()
    w_send(1)

    length = len_ref[0]
    loads[3 * pairs + 3].wait()
    loads[3 * pairs + 4].wait()
    XT[...] = X[...].T
    col_ids = lax.broadcasted_iota(jnp.int32, (1, rows_n), 1)
    visible = jnp.where((col_ids < length) & (GEN[...] == 0), 0.0, -1e9).astype(F32)
    VC[...] = jnp.broadcast_to(visible, (128, rows_n)).T
    QTz[...] = jnp.zeros_like(QTz)
    VT1[...] = jnp.ones_like(VT1)
    for t in range(6, 15):
        loads[t].wait()
    w_forward(0)
    w_send(2)
    w_send(3)
    for i, s in enumerate(others):
        vec_copy(i, s).wait_recv()
    w_ready(0)

    def bias_row(i):
        return jnp.concatenate([VEC[s, i : i + 1, :] for s in range(fsdp)], 1)

    def project(p, part):
        base = p * CHUNK
        if part == 0:
            pr = dot(X[...], W[:, pl.ds(aligned(base, 128), 256)])
            q = (pr[:, :128] + VEC[p, 0:1, :]).astype(BF) * jnp.asarray(0.125, BF)
            qp[p] = q
            KN[p] = pr[:, 128:256].astype(BF)
        if part == 1:
            pr = dot(X[...], W[:, pl.ds(aligned(base + 256, 128), 128)])
            VN[p] = (pr + VEC[p, 1:2, :]).astype(BF)
            qt = qp[p].T
            QTz[2 * p, 0:64, :] = qt[0:64]
            QTz[2 * p + 1, 64:128, :] = qt[64:128]
        if part == 2:
            KT[p] = KN[p].T
            vt = VN[p].T
            VT1[2 * p, 0:64, :] = vt[0:64]
            VT1[2 * p + 1, 0:64, :] = vt[64:128]

    units = HEADS * (rows_n // LB)
    per_head = rows_n // LB
    per_pair = 2 * per_head

    def unit(u):
        return u // per_head, u // per_pair, pl.ds(aligned((u % per_head) * LB, LB), LB)

    def score(u, n):
        h, p, _ = unit(jnp.minimum(u, units - 1))
        b = n % per_head
        raw = dot(KN[p], QTz[h, :, LB * b : LB * b + LB])
        for r in range(per_head):
            rows = slice(LB * r, LB * r + LB)
            w = VC[rows, :]
            part = raw[rows] + jnp.concatenate([w, w], 1)
            if r == b:
                keys = lax.broadcasted_iota(jnp.int32, (LB, LB), 0)
                part = jnp.where(keys == lax.broadcasted_iota(jnp.int32, (LB, LB), 1), raw[rows], part)
            S[rows, LB * (n % 4) : LB * (n % 4) + LB] = part

    def peak(n):
        MX[n % 4, 0:1, :] = jnp.max(S[:, LB * (n % 4) : LB * (n % 4) + LB], axis=0, keepdims=True)

    def weigh(u, n):
        h, p, _ = unit(u)
        b = n % per_head
        v = jnp.exp(S[:, LB * (n % 4) : LB * (n % 4) + LB] - MX[n % 4, 0:1, :]).astype(BF)
        e[h, :, LB * b : LB * b + LB] = v
        slots[n % 2][...] = v

    def mix(u, n):
        h, p, cols = unit(jnp.maximum(u, 0))
        o = dot(VT1[h], slots[n % 2][...])
        r = 1.0 / o[64:65, :]
        rL[h, 0:1, cols] = r
        OT[h, :, cols] = o[0:64, :] * r

    slots = (eb0, eb1)
    for i in range(3):
        project(0, i)
    w_send(pairs)
    score(0, 0)
    score(1, 1)
    peak(0)

    def forward_pair(p, is_last):
        w_forward(pairs if is_last else p + 1)
        for n in range(per_pair):
            if n == 3 and not is_last:
                w_ready(p + 1)
            if not is_last and 3 <= n < 6:
                project(p + 1, n - 3)
            u = per_pair * p + n
            score(u + 2, n + 2)
            weigh(u, n)
            peak(n + 1)
            mix(u - 1, n - 1)
        return 0

    lax.fori_loop(0, pairs - 1, lambda p, _: forward_pair(p, False), 0)
    forward_pair(pairs - 1, True)
    mix(units - 1, per_pair - 1)
    for p in range(pairs):
        ot = jnp.concatenate([OT[2 * p], OT[2 * p + 1]], 0).astype(BF)
        att[:, 128 * p : 128 * p + 128] = ot.T
    w_ready(pairs)
    loads[3 * pairs + 5].wait()

    wo, w1, w2 = (pl.ds((3 + i) * width, width) for i in range(3))
    vecg[...] = jnp.zeros_like(vecg)

    def rows_step(i, _):
        r0 = aligned(i * RB, RB)
        rows = pl.ds(r0, RB)
        gain0, gain1 = bias_row(8), bias_row(9)
        summed = X[rows, :].astype(F32) + dot(att[rows, :], W[:, wo]) + bias_row(2)
        xh1, rs1 = norm(summed)
        normed = xh1 * gain0 + bias_row(5)
        n_low = normed.astype(BF)
        before = dot(n_low, W[:, w1]) + bias_row(3)
        cdf = 0.5 * (1.0 + lax.erf(before * (2.0**-0.5)))
        pdf = jnp.exp(-0.5 * before * before) * (2.0 * jnp.pi) ** -0.5
        a_low = (before * cdf).astype(BF)
        slope = cdf + before * pdf
        second = normed + dot(a_low, W[:, w2]) + bias_row(4)
        xh2, rs2 = norm(second)
        valid = (lax.broadcasted_iota(jnp.int32, (RB, 1), 0) + r0 < length).astype(F32)
        g = COT[rows, :].astype(F32) * valid
        mixed[rows, :] = ((xh2 * gain1 + bias_row(6)) * valid).astype(BF)
        g_second = norm_back(g * gain1, xh2, rs2)
        g_feed = g_second.astype(BF)
        g_before = (slope * dot_t(g_feed, W[:, w2])).astype(BF)
        g_normed = g_second + dot_t(g_before, W[:, w1])
        g_summed = norm_back(g_normed * gain0, xh1, rs1)
        g_branch = g_summed.astype(BF)
        g_att = dot_t(g_branch, W[:, wo]).astype(BF)
        act[rows, :] = a_low
        gf[rows, :] = g_feed
        nl[rows, :] = n_low
        gb[rows, :] = g_before
        gbr[rows, :] = g_branch
        tgrad[rows, :] = g_summed
        vecg[2:3, :] += col_sum(g_branch.astype(F32))
        vecg[3:4, :] += col_sum(g_before.astype(F32))
        vecg[4:5, :] += col_sum(g_feed.astype(F32))
        vecg[5:6, :] += col_sum(g_normed)
        vecg[6:7, :] += col_sum(g)
        vecg[8:9, :] += col_sum(g_normed * xh1)
        vecg[9:10, :] += col_sum(g * xh2)
        for p in range(pairs):
            dAn[p, rows, :] = g_att[:, 128 * p : 128 * p + 128]
        return 0

    lax.fori_loop(0, rows_n // RB, rows_step, 0)
    mixed_copy = pltpu.make_async_copy(mixed, mixed_out, out_sem.at[0])
    mixed_copy.start()

    near, stride = min(2, group), max(group // 2, 1)
    side, place = lax.rem(low, near), lax.div(low, near)
    band = 128 // near
    piece = band // stride
    own_rows = pl.ds(aligned(side * band + place * piece, piece), piece)

    def cell_dev(side_to, place_to, s):
        return (high * group + lax.rem(place_to, stride) * near + side_to, s)

    def cols_of(c):
        if isinstance(c, tuple):
            return 4 + c[0], pl.ds(aligned(4 * width + c[0] * 256, 256), 256)
        return c, pl.ds(c * width, width)

    def s1_all(c):
        i, cols = cols_of(c)
        return [
            remote(G.at[s, :, cols], R1.at[k, :, cols], s1s.at[i, k], s1r.at[i, k], fsdp_dev(s_near))
            for k, s in enumerate((s_near, s_diag))
        ]

    def s1_start(c):
        for copy in s1_all(c):
            copy.start()

    def s2_all(c):
        i, cols = cols_of(c)
        mine = pl.ds(aligned(side * band, band), band)
        other = pl.ds(aligned((near - 1 - side) * band, band), band)
        to = near - 1 - side
        plan = [(s_far, mine, side, s_far)]
        if near > 1:
            plan += [(shard, other, to, shard), (s_far, other, to, s_far)]
        return [
            remote(G.at[s, rows, cols], R2.at[k, :, cols], s2s.at[i, k], s2r.at[i, k], cell_dev(to_side, place, s))
            for k, (s, rows, to_side, _) in enumerate(plan)
        ]

    def s2_start(c):
        pair_sum(c)
        for copy in s2_all(c):
            copy.start()

    def s3_one(c, r):
        i, cols = cols_of(c)
        to = lax.rem(place + r, stride)
        rows = pl.ds(aligned(side * band + to * piece, piece), piece)
        return remote(
            G.at[shard, rows, cols], R3.at[pl.ds((r - 1) * piece, piece), cols], s3s.at[i], s3r.at[i],
            cell_dev(side, place + r, shard),
        )

    def s3_whole(c):
        i, cols = cols_of(c)
        part = R3.at[:, cols]
        return remote(part, part, s3s.at[i], s3r.at[i], cell_dev(side, place + 1, shard))

    def band_sum(c):
        i, cols = cols_of(c)
        mine = pl.ds(aligned(side * band, band), band)
        total = G[shard, mine, cols].astype(F32)
        for k, copy in enumerate(s2_all(c)):
            copy.wait_recv()
            total = total + R2[k, :, cols].astype(F32)
        G[shard, mine, cols] = total.astype(BF)

    def s3_start(c):
        band_sum(c)
        for r in range(1, stride):
            s3_one(c, r).start()

    odd = lax.rem(place, 2)
    beside = place + 1 - 2 * odd
    half = 2 * piece
    half_rows = pl.ds(aligned(side * band + odd * half, half), half)

    def h3_copy(c):
        i, cols = cols_of(c)
        rows = pl.ds(aligned(side * band + (1 - odd) * half, half), half)
        return remote(
            G.at[shard, rows, cols], R3.at[pl.ds(0, half), cols], s3s.at[i], s3r.at[i], cell_dev(side, beside, shard)
        )

    def h3_start(c):
        band_sum(c)
        h3_copy(c).start()

    def h4_copy(c):
        i, cols = cols_of(c)
        return remote(
            G.at[shard, half_rows, cols], R5.at[:, cols], s5s.at[i], s5r.at[i], cell_dev(side, place + 2, shard)
        )

    def h4_start(c):
        i, cols = cols_of(c)
        h3_copy(c).wait_recv()
        G[shard, half_rows, cols] = (
            G[shard, half_rows, cols].astype(F32) + R3[0:half, cols].astype(F32)
        ).astype(BF)
        h4_copy(c).start()

    def h5_all(c):
        i, cols = cols_of(c)
        part = R4.at[half_rows, cols]
        to = near - 1 - side
        return [
            remote(part, part, s4s.at[i], s4r.at[i], cell_dev(a, b, shard))
            for a, b in ((side, beside), (to, place), (to, beside))
        ]

    def h5_whole(c):
        i, cols = cols_of(c)
        part = R4.at[pl.ds(0, 3 * half), cols]
        return remote(part, part, s4s.at[i], s4r.at[i], cell_dev(side, beside, shard))

    def h5_start(c):
        i, cols = cols_of(c)
        h4_copy(c).wait_recv()
        total = G[shard, half_rows, cols].astype(F32) + R5[:, cols].astype(F32)
        R4[half_rows, cols] = total.astype(BF)
        if far > 1:
            for r in range(1, far):
                far_one(c, r, half_rows, half).start()
            for r in range(1, far):
                far_one(c, r, half_rows, half).wait_recv()
                total = total + far_slot(c, r, half)[...].astype(F32)
            for r in range(1, far):
                far_one(c, r, half_rows, half).wait_send()
            R4[half_rows, cols] = total.astype(BF)
        for copy in h5_all(c):
            copy.start()

    def far_slot(c, r, count):
        i, cols = cols_of(c)
        return R3b.at[r - 1, pl.ds(0, count), pl.ds((i % 2) * width, 256 if isinstance(c, tuple) else width)]

    def far_one(c, r, rows, count):
        i, cols = cols_of(c)
        return remote(
            R4.at[rows, cols], far_slot(c, r, count), s3bs.at[i, r - 1], s3br.at[i, r - 1], high_dev(r)
        )

    def s4_one(c, r):
        i, cols = cols_of(c)
        part = R4.at[own_rows, cols]
        return remote(part, part, s4s.at[i], s4r.at[i], low_dev(r))

    def s4_whole(c):
        i, cols = cols_of(c)
        part = R4.at[pl.ds(0, 128 - piece), cols]
        return remote(part, part, s4s.at[i], s4r.at[i], low_dev(1))

    def s4_start(c):
        i, cols = cols_of(c)
        total = G[shard, own_rows, cols].astype(F32)
        s3_whole(c).wait_recv()
        for r in range(1, stride):
            total = total + R3[(r - 1) * piece : r * piece, cols].astype(F32)
        share(c, total)

    def share(c, total):
        i, cols = cols_of(c)
        R4[own_rows, cols] = total.astype(BF)
        if far > 1:
            for r in range(1, far):
                far_one(c, r, own_rows, piece).start()
            for r in range(1, far):
                far_one(c, r, own_rows, piece).wait_recv()
                total = total + far_slot(c, r, piece)[...].astype(F32)
            for r in range(1, far):
                far_one(c, r, own_rows, piece).wait_send()
            R4[own_rows, cols] = total.astype(BF)
        for r in range(1, group):
            s4_one(c, r).start()

    def d_one(c, k, s):
        i, cols = cols_of(c)
        to = lax.rem(low + k, group)
        rows = pl.ds(aligned(lax.rem(to, near) * band + lax.div(to, near) * piece, piece), piece)
        slot = k - 1 if s is shard else group - 1 + k
        which = c[0] - 2
        return remote(
            G.at[s, rows, cols], R6.at[which, slot], s6s.at[which], s6r.at[which], (high * group + to, s)
        )

    def d_all(c):
        return [d_one(c, k, s_far) for k in range(group)] + [d_one(c, k, shard) for k in range(1, group)]

    def d_whole(c):
        which = c[0] - 2
        return remote(R6.at[which], R6.at[which], s6s.at[which], s6r.at[which], low_dev(1))

    def pair_sum(c):
        i, cols = cols_of(c)
        for copy in s1_all(c):
            copy.wait_recv()
        G[s_far, :, cols] = (G[s_far, :, cols].astype(F32) + R1[1, :, cols].astype(F32)).astype(BF)
        G[shard, :, cols] = (G[shard, :, cols].astype(F32) + R1[0, :, cols].astype(F32)).astype(BF)

    def d_start(c):
        pair_sum(c)
        for copy in d_all(c):
            copy.start()

    def d4_start(c):
        i, cols = cols_of(c)
        total = G[shard, own_rows, cols].astype(F32)
        d_whole(c).wait_recv()
        for k in range(2 * group - 1):
            total = total + R6[c[0] - 2, k].astype(F32)
        share(c, total)

    halved = [0, 1, 2, 3, (0,), (1,)]
    direct = [(2,), (3,)]

    def drain():
        for c in halved + direct:
            for copy in s1_all(c):
                copy.wait_send()
        for c in halved:
            for copy in s2_all(c):
                copy.wait_send()
        for c in halved:
            h3_copy(c).wait_send()
            h4_copy(c).wait_send()
            h5_whole(c).wait_send()
        for c in range(parts):
            w_copy(c, shard, 1, fsdp_dev(s_far)).wait_send()
            w_copy(c, shard, 0, fsdp_dev(s_near)).wait_send()
            w_copy(c, s_far, 2, fsdp_dev(s_near)).wait_send()
        for i, s in enumerate(others):
            vec_copy(i, s).wait_send()
            v1_copy(i, s).wait_send()
        for c in direct:
            d_whole(c).wait_send()

    for i, (left, right) in enumerate(((att, gbr), (nl, gb), (act, gf))):
        term = (dot(left[...].T, right[...]) * factor).astype(BF)
        for s in range(fsdp):
            G[s, :, width * i : width * i + width] = term[128 * s : 128 * s + 128, :]
        s1_start(i)
    s2_start(0)

    def prepare(p, _):
        gt = dAn[p].T.astype(F32)
        parts = []
        for hh in range(2):
            h = 2 * p + hh
            x = (gt[64 * hh : 64 * hh + 64, :] * rL[h, 0:1, :]).astype(BF)
            dl[h, 0:1, :] = col_sum(x.astype(F32) * OT[h])
            dATz[h, 64 * hh : 64 * hh + 64, :] = x
            parts.append(x)
        dAn[p] = jnp.concatenate(parts, 0).T
        return 0

    lax.fori_loop(0, pairs, prepare, 0)
    s2_start(1)
    s2_start(2)

    def score_grads(p, hh, n, z_ref):
        cols = pl.ds(n * LB, LB)
        h = 2 * p + hh
        shifted = dot(VN[p], dATz[h, :, cols]) - dl[h, 0:1, cols]
        z_ref[:, cols] = (shifted * e[h, :, cols].astype(F32)).astype(BF)

    def query_grads(p, hh, n, z_ref):
        cols = pl.ds(n * LB, LB)
        half = slice(64 * hh, 64 * hh + 64)
        dQT[lax.rem(p, 2), half, cols] = (dot(KT[p, half, :], z_ref[:, cols]) * 0.125).astype(BF)

    first = lax.broadcasted_iota(jnp.int32, (LB, 128), 1) < 64
    dka = S.at[:, pl.ds(width, 128)]

    def value_grads(p, _):
        cols = pl.ds(aligned(p * CHUNK + 256, 128), 128)
        for n in range(per_head):
            rows = pl.ds(n * LB, LB)
            dv0 = dot(e[2 * p, rows, :], dAn[p])
            dv1 = dot(e[2 * p + 1, rows, :], dAn[p])
            A5[rows, cols] = jnp.where(first, dv0, dv1).astype(BF)
        return 0

    def key_grads(p, hh, n, z_ref):
        rows = pl.ds(n * LB, LB)
        dk = dot(z_ref[rows, :], qp[p])
        if hh == 0:
            dka[rows, :] = dk
        else:
            c = aligned(p * CHUNK, 128)
            A5[rows, pl.ds(c + 128, 128)] = jnp.where(first, dka[rows, :], dk).astype(BF)

    def put_terms(first_col, source):
        term = (dot(XT[...], source) * factor).astype(BF)
        for n in range(fsdp):
            G[n, :, pl.ds(first_col, source.shape[1])] = term[128 * n : 128 * n + 128, :]

    def pair_term(p):
        put_terms(aligned(4 * width + p * 256, 256), A5[:, pl.ds(aligned(p * CHUNK, 128), 256)])

    def pair_end(p):
        c = aligned(p * CHUNK, 128)
        A5[:, pl.ds(c, 128)] = dQT[lax.rem(p, 2)].T
        vecg[0:1, pl.ds(aligned(p * 128, 128), 128)] = col_sum(A5[:, pl.ds(c, 128)].astype(F32))

    lax.fori_loop(0, pairs, value_grads, 0)
    h3_start(0)
    all_dv = jnp.concatenate([A5[:, CHUNK * p + 256 : CHUNK * p + 384] for p in range(pairs)], 1)
    put_terms(3 * width, all_dv)
    s1_start(3)
    vecg[1:2, :] = col_sum(all_dv.astype(F32))

    def backward_pair(p, _):
        opening = isinstance(p, int) and p == 0
        before = p - 1
        for n in range(per_head):
            if not opening:
                key_grads(before, 1, n, Z1)
            if n == 0:
                if not opening:
                    query_grads(before, 1, per_head - 1, Z1)
            else:
                query_grads(p, 0, n - 1, Z0)
            score_grads(p, 0, n, Z0)
        if not opening:
            pair_end(before)
        pl.when(p == 0)(lambda: s2_start(3))
        pl.when(p == 1)(lambda: h3_start(2))
        pl.when(p >= 2)(lambda: s2_start((p - 2,)))
        pl.when(p == 2)(lambda: h3_start(3))
        pl.when(p == 2)(lambda: h4_start(2))
        pl.when(p == 3)(lambda: h3_start((0,)))
        pl.when(p == 3)(lambda: h4_start(3))
        pl.when(p == 3)(lambda: h5_start(2))
        for n in range(per_head):
            key_grads(p, 0, n, Z0)
            if n == 0:
                query_grads(p, 0, per_head - 1, Z0)
            else:
                query_grads(p, 1, n - 1, Z1)
            score_grads(p, 1, n, Z1)
            if n == 0 and not opening:
                pair_term(before)
            if n == 1:
                pl.when(p >= 1)(lambda: s1_start((p - 1,)))
        pl.when(p == 0)(lambda: h3_start(1))
        pl.when(p == 0)(lambda: h4_start(0))
        pl.when(p == 1)(lambda: h4_start(1))
        pl.when(p == 1)(lambda: h5_start(0))
        pl.when(p == 2)(lambda: h5_start(1))
        return 0

    backward_pair(0, 0)
    lax.fori_loop(1, pairs, backward_pair, 0)
    last = pairs - 1
    d_start((2,))
    for n in range(per_head):
        key_grads(last, 1, n, Z1)
    query_grads(last, 1, per_head - 1, Z1)
    pair_end(last)
    pair_term(last)
    s1_start((3,))

    for s in range(fsdp):
        V0[s] = vecg[:, 128 * s : 128 * s + 128] * factor

    def v1_copy(i, s):
        return remote(V0.at[s], VR1.at[i], v1s.at[i], v1r.at[i], fsdp_dev(s))

    def v2_copy(r):
        return remote(V1, VR2.at[r - 1], v2s.at[r - 1], v2r.at[r - 1], low_dev(r))

    def v3_copy(r):
        return remote(V2, VR3.at[r - 1], v3s.at[r - 1], v3r.at[r - 1], high_dev(r))

    for i, s in enumerate(others):
        v1_copy(i, s).start()
    h5_start(3)
    h3_start((1,))
    h4_start((0,))

    def tokens_step(i, _):
        rows = pl.ds(aligned(i * 256, 256), 256)
        tgrad[rows, :] += dot_t(A5[rows, 0 : 3 * width], W[:, 0 : 3 * width])
        return 0

    steps = rows_n // 256
    tokens_step(0, 0)
    d_start((3,))
    lax.fori_loop(1, steps // 2 + 1, tokens_step, 0)
    h4_start((1,))
    h5_start((0,))
    lax.fori_loop(steps // 2 + 1, steps, tokens_step, 0)
    tgrad_copy = pltpu.make_async_copy(tgrad, tgrad_out, out_sem.at[1])
    tgrad_copy.start()
    for i, s in enumerate(others):
        v1_copy(i, s).wait_recv()
    V1[...] = V0[shard] + VR1[0] + VR1[1] + VR1[2]
    for r in range(1, group):
        v2_copy(r).start()
    d4_start((2,))
    h5_start((1,))
    d4_start((3,))
    total = V1[...]
    for r in range(1, group):
        v2_copy(r).wait_recv()
        total = total + VR2[r - 1]
    if far > 1:
        V2[...] = total
        for r in range(1, far):
            v3_copy(r).start()
        for r in range(1, far):
            v3_copy(r).wait_recv()
            total = total + VR3[r - 1]
    VR1[0] = total
    vec_end = pltpu.make_async_copy(VR1.at[0], vec_out, out_sem.at[2])
    vec_end.start()
    drain()
    for c in halved:
        h5_whole(c).wait_recv()
    early = 5 * width
    early_copy = pltpu.make_async_copy(R4.at[:, pl.ds(0, early)], sums_out.at[:, pl.ds(0, early)], out_sem.at[3])
    early_copy.start()
    for c in direct:
        s4_whole(c).wait_recv()
    late_cols = pl.ds(early, width)
    late_copy = pltpu.make_async_copy(R4.at[:, late_cols], sums_out.at[:, late_cols], out_sem.at[4])
    late_copy.start()

    for c in direct:
        s4_whole(c).wait_send()
    for r in range(1, group):
        v2_copy(r).wait_send()
    for r in range(1, far):
        v3_copy(r).wait_send()
    for copy in (mixed_copy, tgrad_copy, vec_end, early_copy, late_copy):
        copy.wait()


def finish_kernel(
    mixed_in, tgrad_in, sums_in, vec_in, mixed_out, tgrad_out, qkv_out, wo_out, w1_out, w2_out, bias_out, gain_out,
    M, T, R, V, Q, O, A, B, bias, gain, sem,
):
    width = M.shape[1]
    pairs = HEADS // 2
    steps = 4
    rows = M.shape[0] // steps
    ins, outs = [], []

    def start(src, dst):
        copy = pltpu.make_async_copy(src, dst, sem.at[len(ins) + len(outs)])
        copy.start()
        return copy

    ins.append(start(sums_in, R))
    ins.append(start(vec_in, V))
    for i in range(steps):
        part = pl.ds(i * rows, rows)
        ins.append(start(tgrad_in.at[part], T.at[part]))
        ins.append(start(mixed_in.at[part], M.at[part]))
    ins[0].wait()
    for p in range(pairs):
        for t in range(2):
            c = 4 * width + 256 * p + 128 * t
            Q[:, t * width + p * 128 : t * width + p * 128 + 128] = R[:, c : c + 128].astype(F32)
    Q[:, 2 * width :] = R[:, 3 * width : 4 * width].astype(F32)
    outs.append(start(Q, qkv_out))
    for i, (ref, to) in enumerate(((O, wo_out), (A, w1_out), (B, w2_out))):
        ref[...] = R[:, i * width : i * width + width].astype(F32)
        outs.append(start(ref, to))
    ins[1].wait()
    bias[...] = V[0:7, :]
    gain[...] = V[8:10, :]
    outs.append(start(bias, bias_out))
    outs.append(start(gain, gain_out))
    for i in range(steps):
        part = pl.ds(i * rows, rows)
        ins[2 + 2 * i].wait()
        outs.append(start(T.at[part], tgrad_out.at[part]))
        ins[3 + 2 * i].wait()
        outs.append(start(M.at[part], mixed_out.at[part]))
    for copy in outs:
        copy.wait()


def call_layer(cells, fsdp, rows_n, width, lengths, generate, *args):
    vm = pl.BlockSpec(memory_space=pltpu.VMEM)
    sm = pl.BlockSpec(memory_space=pltpu.SMEM)
    hb = pl.BlockSpec(memory_space=pl.ANY)
    hbm = pl.BlockSpec(memory_space=pltpu.HBM)
    shard_rows = width // fsdp
    group = min(GROUP, cells)
    far = cells // group
    near = min(2, group)
    stride = group // near
    band, piece = 128 // near, 128 // group
    factor = 1.0 / (cells * fsdp)
    dma = pltpu.SemaphoreType.DMA
    outs = (((rows_n, width), BF), ((rows_n, width), F32), ((128, 6 * width), BF), ((16, 128), F32))
    far_n = max(far - 1, 1)
    LB = 256
    scratch = [
        ((rows_n, width), BF), ((rows_n, width), BF), ((1, rows_n), jnp.int32),
        ((width, 6 * width), BF), ((fsdp, 16, 128), F32), ((width, rows_n), BF), ((rows_n, 128), F32),
        ((4, rows_n, 128), BF), ((8, 128, rows_n), BF), ((4, rows_n, 128), BF), ((4, 128, rows_n), BF),
        ((4, rows_n, 128), BF), ((8, 80, rows_n), BF), ((8, rows_n, rows_n), BF),
        ((rows_n, width), BF), ((8, 64, rows_n), F32), ((8, 8, rows_n), F32), ((rows_n, 5 * width), BF),
        ((4, rows_n, 128), BF), ((8, 8, rows_n), F32), ((rows_n, rows_n), BF), ((rows_n, rows_n), BF),
        ((2, 128, rows_n), BF),
        ((rows_n, 4 * LB), F32), ((4, 8, LB), F32), ((rows_n, LB), BF), ((rows_n, LB), BF),
        ((16, width), F32),
        ((fsdp, 128, 6 * width), BF), ((2, 128, 6 * width), BF), ((2 * near - 1, band, 6 * width), BF),
        (((stride - 1) * piece, 6 * width), BF), ((far_n, 2 * piece, 2 * width), BF), ((128, 6 * width), BF),
        ((2 * piece, 6 * width), BF), ((2, 2 * group - 1, piece, 256), BF),
        ((fsdp, 16, 128), F32), ((fsdp - 1, 16, 128), F32), ((16, 128), F32), ((group - 1, 16, 128), F32),
        ((16, 128), F32), ((far_n, 16, 128), F32),
    ]
    sems = [
        (18,), (5,), (5, 3), (5, 3), (3,), (3,), (8, 2), (8, 2), (8, 2 * near - 1), (8, 2 * near - 1), (8,), (8,),
        (8, far_n), (8, far_n), (8,), (8,), (8,), (8,), (2,), (2,), (3,), (3,), (group - 1,), (group - 1,), (far_n,), (far_n,),
    ]
    results = pl.pallas_call(
        functools.partial(layer_kernel, cells, fsdp, factor),
        out_shape=[jax.ShapeDtypeStruct(s, t) for s, t in outs],
        in_specs=[sm] + [hb] * 7 + [vm] * 2,
        out_specs=[hb] * 4,
        scratch_shapes=[pltpu.VMEM(s, t) for s, t in scratch] + [dma(s) for s in sems],
        compiler_params=pltpu.CompilerParams(
            vmem_limit_bytes=63 * 2**20 + 2**19, collective_id=0, has_side_effects=True
        ),
        name="layer",
    )(lengths, generate, *args)
    finals = (
        ((rows_n, width), BF), ((rows_n, width), F32), ((shard_rows, 3 * width), F32), ((shard_rows, width), F32),
        ((shard_rows, width), F32), ((shard_rows, width), F32), ((7, width // fsdp), F32), ((2, width // fsdp), F32),
    )
    buffers = list(outs) + list(finals[2:])
    return pl.pallas_call(
        finish_kernel,
        out_shape=[jax.ShapeDtypeStruct(s, t) for s, t in finals],
        in_specs=[hbm] * 4,
        out_specs=[hbm] * 8,
        scratch_shapes=[pltpu.VMEM(s, t) for s, t in buffers] + [dma((24,))],
        compiler_params=pltpu.CompilerParams(vmem_limit_bytes=63 * 2**20),
        name="finish",
    )(*results)


def body(cells, fsdp, tokens, cotangent, lengths, generate, *weights):
    _, rows_n, width = tokens.shape
    mixed, tokens_grad, *grads = call_layer(
        cells, fsdp, rows_n, width, lengths, generate, tokens[0], cotangent[0], *weights
    )
    return (mixed[None], tokens_grad[None], *grads)


def solution(mesh):
    split = P(("cells", "fsdp"), None, None)
    rows, cols = P("fsdp", None), P(None, "fsdp")
    return jax.shard_map(
        functools.partial(body, mesh.shape["cells"], mesh.shape["fsdp"]),
        mesh=mesh,
        in_specs=(split, split, P(("cells", "fsdp")), P(("cells", "fsdp"), None), rows, rows, rows, rows, cols, cols),
        out_specs=(split, split, rows, rows, rows, rows, cols, cols),
        check_vma=False,
    )
```

```python
import functools

import jax
import jax.numpy as jnp
from jax import lax
from jax.experimental import pallas as pl
from jax.experimental.pallas import tpu as pltpu
from jax.sharding import PartitionSpec as P

F32, BF = jnp.float32, jnp.bfloat16
MESH = pl.DeviceIdType.MESH
HEADS = 8
EPS = 1e-5
CHUNK = 384
GROUP = 8


def dot(a, b):
    return jnp.dot(a, b, preferred_element_type=F32)


def dot_t(a, b):
    return lax.dot_general(a, b, (((1,), (1,)), ((), ())), preferred_element_type=F32)


def col_sum(v):
    return jnp.sum(v, axis=0, keepdims=True)


def norm(v):
    centred = v - jnp.mean(v, axis=1, keepdims=True)
    r = lax.rsqrt(jnp.mean(centred * centred, axis=1, keepdims=True) + EPS)
    return centred * r, r


def norm_back(g, xhat, r):
    g_mean = jnp.mean(g, axis=1, keepdims=True)
    x_mean = jnp.mean(g * xhat, axis=1, keepdims=True)
    return r * (g - g_mean - xhat * x_mean)


def aligned(value, step):
    return pl.multiple_of(value, step)


def layer_kernel(
    cells, fsdp, factor,
    len_ref, gen_in, tok_in, cot_in, wq_in, wo_in, w1_in, w2_in, bias_in, gain_in,
    mixed_out, tgrad_out, sums_out, vec_out,
    X, COT, GEN, W, VEC, XT, VC, qp, QTz, KN, KT, VN, VT1, e, att, OT, rL, A5, dAn, dl, Z0, Z1, dQT,
    S, MX, eb0, eb1, vecg,
    G, R1, R2, R3, R3b, R4, R5, R6, V0, VR1, V1, VR2, V2, VR3,
    in_sem, out_sem, gs_sem, gr_sem, vs_sem, vr_sem,
    s1s, s1r, s2s, s2r, s3s, s3r, s3bs, s3br, s4s, s4r, s5s, s5r, s6s, s6r, v1s, v1r, v2s, v2r, v3s, v3r,
):
    rows_n, width = X.shape
    pairs = HEADS // 2
    RB = 512
    LB = 256
    cell = lax.axis_index("cells")
    shard = lax.axis_index("fsdp")
    group = min(GROUP, cells)
    far = cells // group
    low = lax.rem(cell, group)
    high = lax.div(cell, group)
    act, gf, nl, gb, gbr = (A5.at[:, pl.ds(i * width, width)] for i in range(5))
    dATz, mixed, tgrad = QTz, COT, S.at[:, pl.ds(0, width)]

    def near_shard(s):
        return s + 1 - 2 * lax.rem(s, 2)

    def far_shard(s):
        return s + 2 - 4 * lax.rem(lax.div(s, 2), 2)

    def fsdp_dev(s):
        return (cell, s)

    def low_dev(r):
        return (high * group + lax.rem(low + r, group), shard)

    def high_dev(r):
        return (lax.rem(high + r, far) * group + low, shard)

    s_near, s_far = near_shard(shard), far_shard(shard)
    s_diag = near_shard(s_far)
    others = (s_near, s_far, s_diag)

    def remote(src, dst, send, recv, device):
        return pltpu.make_async_remote_copy(
            src_ref=src, dst_ref=dst, send_sem=send, recv_sem=recv, device_id=device, device_id_type=MESH
        )

    barrier = pltpu.get_barrier_semaphore()
    for s in others:
        pl.semaphore_signal(barrier, inc=1, device_id=fsdp_dev(s), device_id_type=MESH)
    for r in range(1, group):
        pl.semaphore_signal(barrier, inc=1, device_id=low_dev(r), device_id_type=MESH)
    for r in range(1, group):
        pl.semaphore_signal(barrier, inc=1, device_id=(low_dev(r)[0], s_far), device_id_type=MESH)
    for r in range(1, far):
        pl.semaphore_signal(barrier, inc=1, device_id=high_dev(r), device_id_type=MESH)

    own = pl.ds(aligned(shard * 128, 128), 128)
    loads = []
    for p in range(pairs):
        for t in range(3):
            loads.append((wq_in.at[:, pl.ds(t * width + p * 128, 128)], W.at[own, pl.ds(p * CHUNK + t * 128, 128)]))
    for i, ref in enumerate((wo_in, w1_in, w2_in)):
        loads.append((ref, W.at[own, pl.ds((3 + i) * width, width)]))
    loads += [(tok_in, X), (gen_in, GEN), (cot_in, COT)]
    loads = [pltpu.make_async_copy(a, b, in_sem.at[i]) for i, (a, b) in enumerate(loads)]
    for copy in loads:
        copy.start()
    VEC[shard] = jnp.zeros((16, 128), F32)
    VEC[shard, 0:7, :] = bias_in[...].astype(F32)
    VEC[shard, 8:10, :] = gain_in[...].astype(F32)

    def w_copy(c, owner, hop, device):
        whole = isinstance(c, int) and c == pairs
        cols = pl.ds(3 * width, 3 * width) if whole else pl.ds(aligned(c * CHUNK, 128), CHUNK)
        part = W.at[pl.ds(aligned(owner * 128, 128), 128), cols]
        return remote(part, part, gs_sem.at[c, hop], gr_sem.at[c, hop], device)

    def vec_copy(i, s):
        return remote(VEC.at[shard], VEC.at[shard], vs_sem.at[i], vr_sem.at[i], fsdp_dev(s))

    parts = pairs + 1

    def w_send(c):
        w_copy(c, shard, 1, fsdp_dev(s_far)).start()
        w_copy(c, shard, 0, fsdp_dev(s_near)).start()

    def w_forward(c):
        w_copy(c, shard, 1, fsdp_dev(s_far)).wait_recv()
        w_copy(c, s_far, 2, fsdp_dev(s_near)).start()

    def w_ready(c):
        w_copy(c, shard, 0, fsdp_dev(s_near)).wait_recv()
        w_copy(c, s_far, 2, fsdp_dev(s_near)).wait_recv()

    for t in range(3):
        loads[t].wait()
    pl.semaphore_wait(barrier, fsdp - 1 + 2 * (group - 1) + far - 1)
    w_send(0)
    for i, s in enumerate(others):
        vec_copy(i, s).start()
    for t in range(3, 6):
        loads[t].wait()
    w_send(1)

    length = len_ref[0]
    loads[3 * pairs + 3].wait()
    loads[3 * pairs + 4].wait()
    XT[...] = X[...].T
    col_ids = lax.broadcasted_iota(jnp.int32, (1, rows_n), 1)
    visible = jnp.where((col_ids < length) & (GEN[...] == 0), 0.0, -1e9).astype(F32)
    VC[...] = jnp.broadcast_to(visible, (128, rows_n)).T
    QTz[...] = jnp.zeros_like(QTz)
    VT1[...] = jnp.ones_like(VT1)
    for t in range(6, 15):
        loads[t].wait()
    w_forward(0)
    w_send(2)
    w_send(3)
    for i, s in enumerate(others):
        vec_copy(i, s).wait_recv()
    w_ready(0)

    def bias_row(i):
        return jnp.concatenate([VEC[s, i : i + 1, :] for s in range(fsdp)], 1)

    def project(p, part):
        base = p * CHUNK
        if part == 0:
            pr = dot(X[...], W[:, pl.ds(aligned(base, 128), 256)])
            q = (pr[:, :128] + VEC[p, 0:1, :]).astype(BF) * jnp.asarray(0.125, BF)
            qp[p] = q
            KN[p] = pr[:, 128:256].astype(BF)
        if part == 1:
            pr = dot(X[...], W[:, pl.ds(aligned(base + 256, 128), 128)])
            VN[p] = (pr + VEC[p, 1:2, :]).astype(BF)
            qt = qp[p].T
            QTz[2 * p, 0:64, :] = qt[0:64]
            QTz[2 * p + 1, 64:128, :] = qt[64:128]
        if part == 2:
            KT[p] = KN[p].T
            vt = VN[p].T
            VT1[2 * p, 0:64, :] = vt[0:64]
            VT1[2 * p + 1, 0:64, :] = vt[64:128]

    units = HEADS * (rows_n // LB)
    per_head = rows_n // LB
    per_pair = 2 * per_head

    def unit(u):
        return u // per_head, u // per_pair, pl.ds(aligned((u % per_head) * LB, LB), LB)

    def score(u, n):
        h, p, _ = unit(jnp.minimum(u, units - 1))
        b = n % per_head
        raw = dot(KN[p], QTz[h, :, LB * b : LB * b + LB])
        for r in range(per_head):
            rows = slice(LB * r, LB * r + LB)
            w = VC[rows, :]
            part = raw[rows] + jnp.concatenate([w, w], 1)
            if r == b:
                keys = lax.broadcasted_iota(jnp.int32, (LB, LB), 0)
                part = jnp.where(keys == lax.broadcasted_iota(jnp.int32, (LB, LB), 1), raw[rows], part)
            S[rows, LB * (n % 4) : LB * (n % 4) + LB] = part

    def peak(n):
        MX[n % 4, 0:1, :] = jnp.max(S[:, LB * (n % 4) : LB * (n % 4) + LB], axis=0, keepdims=True)

    def weigh(u, n):
        h, p, _ = unit(u)
        b = n % per_head
        v = jnp.exp(S[:, LB * (n % 4) : LB * (n % 4) + LB] - MX[n % 4, 0:1, :]).astype(BF)
        e[h, :, LB * b : LB * b + LB] = v
        slots[n % 2][...] = v

    def mix(u, n):
        h, p, cols = unit(jnp.maximum(u, 0))
        o = dot(VT1[h], slots[n % 2][...])
        r = 1.0 / o[64:65, :]
        rL[h, 0:1, cols] = r
        OT[h, :, cols] = o[0:64, :] * r

    slots = (eb0, eb1)
    for i in range(3):
        project(0, i)
    w_send(pairs)
    score(0, 0)
    score(1, 1)
    peak(0)

    def forward_pair(p, is_last):
        w_forward(pairs if is_last else p + 1)
        for n in range(per_pair):
            if n == 3 and not is_last:
                w_ready(p + 1)
            if not is_last and 3 <= n < 6:
                project(p + 1, n - 3)
            u = per_pair * p + n
            score(u + 2, n + 2)
            weigh(u, n)
            peak(n + 1)
            mix(u - 1, n - 1)
        return 0

    lax.fori_loop(0, pairs - 1, lambda p, _: forward_pair(p, False), 0)
    forward_pair(pairs - 1, True)
    mix(units - 1, per_pair - 1)
    for p in range(pairs):
        ot = jnp.concatenate([OT[2 * p], OT[2 * p + 1]], 0).astype(BF)
        att[:, 128 * p : 128 * p + 128] = ot.T
    w_ready(pairs)
    loads[3 * pairs + 5].wait()

    wo, w1, w2 = (pl.ds((3 + i) * width, width) for i in range(3))
    vecg[...] = jnp.zeros_like(vecg)

    def rows_step(i, _):
        r0 = aligned(i * RB, RB)
        rows = pl.ds(r0, RB)
        gain0, gain1 = bias_row(8), bias_row(9)
        summed = X[rows, :].astype(F32) + dot(att[rows, :], W[:, wo]) + bias_row(2)
        xh1, rs1 = norm(summed)
        normed = xh1 * gain0 + bias_row(5)
        n_low = normed.astype(BF)
        before = dot(n_low, W[:, w1]) + bias_row(3)
        cdf = 0.5 * (1.0 + lax.erf(before * (2.0**-0.5)))
        pdf = jnp.exp(-0.5 * before * before) * (2.0 * jnp.pi) ** -0.5
        a_low = (before * cdf).astype(BF)
        slope = cdf + before * pdf
        second = normed + dot(a_low, W[:, w2]) + bias_row(4)
        xh2, rs2 = norm(second)
        valid = (lax.broadcasted_iota(jnp.int32, (RB, 1), 0) + r0 < length).astype(F32)
        g = COT[rows, :].astype(F32) * valid
        mixed[rows, :] = ((xh2 * gain1 + bias_row(6)) * valid).astype(BF)
        g_second = norm_back(g * gain1, xh2, rs2)
        g_feed = g_second.astype(BF)
        g_before = (slope * dot_t(g_feed, W[:, w2])).astype(BF)
        g_normed = g_second + dot_t(g_before, W[:, w1])
        g_summed = norm_back(g_normed * gain0, xh1, rs1)
        g_branch = g_summed.astype(BF)
        g_att = dot_t(g_branch, W[:, wo]).astype(BF)
        act[rows, :] = a_low
        gf[rows, :] = g_feed
        nl[rows, :] = n_low
        gb[rows, :] = g_before
        gbr[rows, :] = g_branch
        tgrad[rows, :] = g_summed
        vecg[2:3, :] += col_sum(g_branch.astype(F32))
        vecg[3:4, :] += col_sum(g_before.astype(F32))
        vecg[4:5, :] += col_sum(g_feed.astype(F32))
        vecg[5:6, :] += col_sum(g_normed)
        vecg[6:7, :] += col_sum(g)
        vecg[8:9, :] += col_sum(g_normed * xh1)
        vecg[9:10, :] += col_sum(g * xh2)
        for p in range(pairs):
            dAn[p, rows, :] = g_att[:, 128 * p : 128 * p + 128]
        return 0

    lax.fori_loop(0, rows_n // RB, rows_step, 0)
    mixed_copy = pltpu.make_async_copy(mixed, mixed_out, out_sem.at[0])
    mixed_copy.start()

    near, stride = min(2, group), max(group // 2, 1)
    side, place = lax.rem(low, near), lax.div(low, near)
    band = 128 // near
    piece = band // stride
    own_rows = pl.ds(aligned(side * band + place * piece, piece), piece)

    def cell_dev(side_to, place_to, s):
        return (high * group + lax.rem(place_to, stride) * near + side_to, s)

    def cols_of(c):
        if isinstance(c, tuple):
            return 4 + c[0], pl.ds(aligned(4 * width + c[0] * 256, 256), 256)
        return c, pl.ds(c * width, width)

    def s1_all(c):
        i, cols = cols_of(c)
        return [
            remote(G.at[s, :, cols], R1.at[k, :, cols], s1s.at[i, k], s1r.at[i, k], fsdp_dev(s_near))
            for k, s in enumerate((s_near, s_diag))
        ]

    def s1_start(c):
        for copy in s1_all(c):
            copy.start()

    def s2_all(c):
        i, cols = cols_of(c)
        mine = pl.ds(aligned(side * band, band), band)
        other = pl.ds(aligned((near - 1 - side) * band, band), band)
        to = near - 1 - side
        plan = [(s_far, mine, side, s_far)]
        if near > 1:
            plan += [(shard, other, to, shard), (s_far, other, to, s_far)]
        return [
            remote(G.at[s, rows, cols], R2.at[k, :, cols], s2s.at[i, k], s2r.at[i, k], cell_dev(to_side, place, s))
            for k, (s, rows, to_side, _) in enumerate(plan)
        ]

    def s2_start(c):
        pair_sum(c)
        for copy in s2_all(c):
            copy.start()

    def s3_one(c, r):
        i, cols = cols_of(c)
        to = lax.rem(place + r, stride)
        rows = pl.ds(aligned(side * band + to * piece, piece), piece)
        return remote(
            G.at[shard, rows, cols], R3.at[pl.ds((r - 1) * piece, piece), cols], s3s.at[i], s3r.at[i],
            cell_dev(side, place + r, shard),
        )

    def s3_whole(c):
        i, cols = cols_of(c)
        part = R3.at[:, cols]
        return remote(part, part, s3s.at[i], s3r.at[i], cell_dev(side, place + 1, shard))

    def band_sum(c):
        i, cols = cols_of(c)
        mine = pl.ds(aligned(side * band, band), band)
        total = G[shard, mine, cols].astype(F32)
        for k, copy in enumerate(s2_all(c)):
            copy.wait_recv()
            total = total + R2[k, :, cols].astype(F32)
        G[shard, mine, cols] = total.astype(BF)

    def s3_start(c):
        band_sum(c)
        for r in range(1, stride):
            s3_one(c, r).start()

    odd = lax.rem(place, 2)
    beside = place + 1 - 2 * odd
    half = 2 * piece
    half_rows = pl.ds(aligned(side * band + odd * half, half), half)

    def h3_copy(c):
        i, cols = cols_of(c)
        rows = pl.ds(aligned(side * band + (1 - odd) * half, half), half)
        return remote(
            G.at[shard, rows, cols], R3.at[pl.ds(0, half), cols], s3s.at[i], s3r.at[i], cell_dev(side, beside, shard)
        )

    def h3_start(c):
        band_sum(c)
        h3_copy(c).start()

    def h4_copy(c):
        i, cols = cols_of(c)
        return remote(
            G.at[shard, half_rows, cols], R5.at[:, cols], s5s.at[i], s5r.at[i], cell_dev(side, place + 2, shard)
        )

    def h4_start(c):
        i, cols = cols_of(c)
        h3_copy(c).wait_recv()
        G[shard, half_rows, cols] = (
            G[shard, half_rows, cols].astype(F32) + R3[0:half, cols].astype(F32)
        ).astype(BF)
        h4_copy(c).start()

    def h5_all(c):
        i, cols = cols_of(c)
        part = R4.at[half_rows, cols]
        to = near - 1 - side
        return [
            remote(part, part, s4s.at[i], s4r.at[i], cell_dev(a, b, shard))
            for a, b in ((side, beside), (to, place), (to, beside))
        ]

    def h5_whole(c):
        i, cols = cols_of(c)
        part = R4.at[pl.ds(0, 3 * half), cols]
        return remote(part, part, s4s.at[i], s4r.at[i], cell_dev(side, beside, shard))

    def h5_start(c):
        i, cols = cols_of(c)
        h4_copy(c).wait_recv()
        total = G[shard, half_rows, cols].astype(F32) + R5[:, cols].astype(F32)
        R4[half_rows, cols] = total.astype(BF)
        if far > 1:
            for r in range(1, far):
                far_one(c, r, half_rows, half).start()
            for r in range(1, far):
                far_one(c, r, half_rows, half).wait_recv()
                total = total + far_slot(c, r, half)[...].astype(F32)
            for r in range(1, far):
                far_one(c, r, half_rows, half).wait_send()
            R4[half_rows, cols] = total.astype(BF)
        for copy in h5_all(c):
            copy.start()

    def far_slot(c, r, count):
        i, cols = cols_of(c)
        return R3b.at[r - 1, pl.ds(0, count), pl.ds((i % 2) * width, 256 if isinstance(c, tuple) else width)]

    def far_one(c, r, rows, count):
        i, cols = cols_of(c)
        return remote(
            R4.at[rows, cols], far_slot(c, r, count), s3bs.at[i, r - 1], s3br.at[i, r - 1], high_dev(r)
        )

    def s4_one(c, r):
        i, cols = cols_of(c)
        part = R4.at[own_rows, cols]
        return remote(part, part, s4s.at[i], s4r.at[i], low_dev(r))

    def s4_whole(c):
        i, cols = cols_of(c)
        part = R4.at[pl.ds(0, 128 - piece), cols]
        return remote(part, part, s4s.at[i], s4r.at[i], low_dev(1))

    def s4_start(c):
        i, cols = cols_of(c)
        total = G[shard, own_rows, cols].astype(F32)
        s3_whole(c).wait_recv()
        for r in range(1, stride):
            total = total + R3[(r - 1) * piece : r * piece, cols].astype(F32)
        share(c, total)

    def share(c, total):
        i, cols = cols_of(c)
        R4[own_rows, cols] = total.astype(BF)
        if far > 1:
            for r in range(1, far):
                far_one(c, r, own_rows, piece).start()
            for r in range(1, far):
                far_one(c, r, own_rows, piece).wait_recv()
                total = total + far_slot(c, r, piece)[...].astype(F32)
            for r in range(1, far):
                far_one(c, r, own_rows, piece).wait_send()
            R4[own_rows, cols] = total.astype(BF)
        for r in range(1, group):
            s4_one(c, r).start()

    def d_one(c, k, s):
        i, cols = cols_of(c)
        to = lax.rem(low + k, group)
        rows = pl.ds(aligned(lax.rem(to, near) * band + lax.div(to, near) * piece, piece), piece)
        slot = k - 1 if s is shard else group - 1 + k
        which = c[0] - 2
        return remote(
            G.at[s, rows, cols], R6.at[which, slot], s6s.at[which], s6r.at[which], (high * group + to, s)
        )

    def d_all(c):
        return [d_one(c, k, s_far) for k in range(group)] + [d_one(c, k, shard) for k in range(1, group)]

    def d_whole(c):
        which = c[0] - 2
        return remote(R6.at[which], R6.at[which], s6s.at[which], s6r.at[which], low_dev(1))

    def pair_sum(c):
        i, cols = cols_of(c)
        for copy in s1_all(c):
            copy.wait_recv()
        G[s_far, :, cols] = (G[s_far, :, cols].astype(F32) + R1[1, :, cols].astype(F32)).astype(BF)
        G[shard, :, cols] = (G[shard, :, cols].astype(F32) + R1[0, :, cols].astype(F32)).astype(BF)

    def d_start(c):
        pair_sum(c)
        for copy in d_all(c):
            copy.start()

    def d4_start(c):
        i, cols = cols_of(c)
        total = G[shard, own_rows, cols].astype(F32)
        d_whole(c).wait_recv()
        for k in range(2 * group - 1):
            total = total + R6[c[0] - 2, k].astype(F32)
        share(c, total)

    halved = [0, 1, 2, 3, (0,), (1,)]
    direct = [(2,), (3,)]

    def drain():
        for c in halved + direct:
            for copy in s1_all(c):
                copy.wait_send()
        for c in halved:
            for copy in s2_all(c):
                copy.wait_send()
        for c in halved:
            h3_copy(c).wait_send()
            h4_copy(c).wait_send()
            h5_whole(c).wait_send()
        for c in range(parts):
            w_copy(c, shard, 1, fsdp_dev(s_far)).wait_send()
            w_copy(c, shard, 0, fsdp_dev(s_near)).wait_send()
            w_copy(c, s_far, 2, fsdp_dev(s_near)).wait_send()
        for i, s in enumerate(others):
            vec_copy(i, s).wait_send()
            v1_copy(i, s).wait_send()
        for c in direct:
            d_whole(c).wait_send()

    for i, (left, right) in enumerate(((att, gbr), (nl, gb), (act, gf))):
        term = (dot(left[...].T, right[...]) * factor).astype(BF)
        for s in range(fsdp):
            G[s, :, width * i : width * i + width] = term[128 * s : 128 * s + 128, :]
        s1_start(i)
    s2_start(0)

    def prepare(p, _):
        gt = dAn[p].T.astype(F32)
        parts = []
        for hh in range(2):
            h = 2 * p + hh
            x = (gt[64 * hh : 64 * hh + 64, :] * rL[h, 0:1, :]).astype(BF)
            dl[h, 0:1, :] = col_sum(x.astype(F32) * OT[h])
            dATz[h, 64 * hh : 64 * hh + 64, :] = x
            parts.append(x)
        dAn[p] = jnp.concatenate(parts, 0).T
        return 0

    lax.fori_loop(0, pairs, prepare, 0)
    s2_start(1)
    s2_start(2)

    def score_grads(p, hh, n, z_ref):
        cols = pl.ds(n * LB, LB)
        h = 2 * p + hh
        shifted = dot(VN[p], dATz[h, :, cols]) - dl[h, 0:1, cols]
        z_ref[:, cols] = (shifted * e[h, :, cols].astype(F32)).astype(BF)

    def query_grads(p, hh, n, z_ref):
        cols = pl.ds(n * LB, LB)
        half = slice(64 * hh, 64 * hh + 64)
        dQT[lax.rem(p, 2), half, cols] = (dot(KT[p, half, :], z_ref[:, cols]) * 0.125).astype(BF)

    first = lax.broadcasted_iota(jnp.int32, (LB, 128), 1) < 64
    dka = S.at[:, pl.ds(width, 128)]

    def value_grads(p, _):
        cols = pl.ds(aligned(p * CHUNK + 256, 128), 128)
        wide = lax.broadcasted_iota(jnp.int32, (2 * LB, 128), 1) < 64
        for n in range(per_head // 2):
            rows = pl.ds(n * 2 * LB, 2 * LB)
            dv0 = dot(e[2 * p, rows, :], dAn[p])
            dv1 = dot(e[2 * p + 1, rows, :], dAn[p])
            A5[rows, cols] = jnp.where(wide, dv0, dv1).astype(BF)
        return 0

    def key_grads(p, hh, n, z_ref):
        rows = pl.ds(n * LB, LB)
        dk = dot(z_ref[rows, :], qp[p])
        if hh == 0:
            dka[rows, :] = dk
        else:
            c = aligned(p * CHUNK, 128)
            A5[rows, pl.ds(c + 128, 128)] = jnp.where(first, dka[rows, :], dk).astype(BF)

    def put_terms(first_col, source):
        term = (dot(XT[...], source) * factor).astype(BF)
        for n in range(fsdp):
            G[n, :, pl.ds(first_col, source.shape[1])] = term[128 * n : 128 * n + 128, :]

    def pair_term(p):
        put_terms(aligned(4 * width + p * 256, 256), A5[:, pl.ds(aligned(p * CHUNK, 128), 256)])

    def pair_end(p):
        c = aligned(p * CHUNK, 128)
        A5[:, pl.ds(c, 128)] = dQT[lax.rem(p, 2)].T
        vecg[0:1, pl.ds(aligned(p * 128, 128), 128)] = col_sum(A5[:, pl.ds(c, 128)].astype(F32))

    lax.fori_loop(0, pairs, value_grads, 0)
    h3_start(0)
    all_dv = jnp.concatenate([A5[:, CHUNK * p + 256 : CHUNK * p + 384] for p in range(pairs)], 1)
    put_terms(3 * width, all_dv)
    s1_start(3)
    vecg[1:2, :] = col_sum(all_dv.astype(F32))

    def backward_pair(p, _):
        opening = isinstance(p, int) and p == 0
        before = p - 1
        for n in range(per_head):
            if not opening:
                key_grads(before, 1, n, Z1)
            if n == 0:
                if not opening:
                    query_grads(before, 1, per_head - 1, Z1)
            else:
                query_grads(p, 0, n - 1, Z0)
            score_grads(p, 0, n, Z0)
        if not opening:
            pair_end(before)
        pl.when(p == 0)(lambda: s2_start(3))
        pl.when(p == 1)(lambda: h3_start(2))
        pl.when(p >= 2)(lambda: s2_start((p - 2,)))
        pl.when(p == 2)(lambda: h3_start(3))
        pl.when(p == 2)(lambda: h4_start(2))
        pl.when(p == 3)(lambda: h3_start((0,)))
        pl.when(p == 3)(lambda: h4_start(3))
        pl.when(p == 3)(lambda: h5_start(2))
        for n in range(per_head):
            key_grads(p, 0, n, Z0)
            if n == 0:
                query_grads(p, 0, per_head - 1, Z0)
            else:
                query_grads(p, 1, n - 1, Z1)
            score_grads(p, 1, n, Z1)
            if n == 0 and not opening:
                pair_term(before)
            if n == 1:
                pl.when(p >= 1)(lambda: s1_start((p - 1,)))
        pl.when(p == 0)(lambda: h3_start(1))
        pl.when(p == 0)(lambda: h4_start(0))
        pl.when(p == 1)(lambda: h4_start(1))
        pl.when(p == 1)(lambda: h5_start(0))
        pl.when(p == 2)(lambda: h5_start(1))
        return 0

    backward_pair(0, 0)
    lax.fori_loop(1, pairs, backward_pair, 0)
    last = pairs - 1
    d_start((2,))
    for n in range(per_head):
        key_grads(last, 1, n, Z1)
    query_grads(last, 1, per_head - 1, Z1)
    pair_end(last)
    pair_term(last)
    s1_start((3,))

    for s in range(fsdp):
        V0[s] = vecg[:, 128 * s : 128 * s + 128] * factor

    def v1_copy(i, s):
        return remote(V0.at[s], VR1.at[i], v1s.at[i], v1r.at[i], fsdp_dev(s))

    def v2_copy(r):
        return remote(V1, VR2.at[r - 1], v2s.at[r - 1], v2r.at[r - 1], low_dev(r))

    def v3_copy(r):
        return remote(V2, VR3.at[r - 1], v3s.at[r - 1], v3r.at[r - 1], high_dev(r))

    for i, s in enumerate(others):
        v1_copy(i, s).start()
    h5_start(3)
    h3_start((1,))
    h4_start((0,))

    def tokens_step(i, _):
        rows = pl.ds(aligned(i * 256, 256), 256)
        tgrad[rows, :] += dot_t(A5[rows, 0 : 3 * width], W[:, 0 : 3 * width])
        return 0

    steps = rows_n // 256
    tokens_step(0, 0)
    d_start((3,))
    lax.fori_loop(1, steps // 2 + 1, tokens_step, 0)
    h4_start((1,))
    h5_start((0,))
    lax.fori_loop(steps // 2 + 1, steps, tokens_step, 0)
    tgrad_copy = pltpu.make_async_copy(tgrad, tgrad_out, out_sem.at[1])
    tgrad_copy.start()
    for i, s in enumerate(others):
        v1_copy(i, s).wait_recv()
    V1[...] = V0[shard] + VR1[0] + VR1[1] + VR1[2]
    for r in range(1, group):
        v2_copy(r).start()
    d4_start((2,))
    h5_start((1,))
    d4_start((3,))
    total = V1[...]
    for r in range(1, group):
        v2_copy(r).wait_recv()
        total = total + VR2[r - 1]
    if far > 1:
        V2[...] = total
        for r in range(1, far):
            v3_copy(r).start()
        for r in range(1, far):
            v3_copy(r).wait_recv()
            total = total + VR3[r - 1]
    VR1[0] = total
    vec_end = pltpu.make_async_copy(VR1.at[0], vec_out, out_sem.at[2])
    vec_end.start()
    drain()
    for c in halved:
        h5_whole(c).wait_recv()
    early = 5 * width
    early_copy = pltpu.make_async_copy(R4.at[:, pl.ds(0, early)], sums_out.at[:, pl.ds(0, early)], out_sem.at[3])
    early_copy.start()
    for c in direct:
        s4_whole(c).wait_recv()
    late_cols = pl.ds(early, width)
    late_copy = pltpu.make_async_copy(R4.at[:, late_cols], sums_out.at[:, late_cols], out_sem.at[4])
    late_copy.start()

    for c in direct:
        s4_whole(c).wait_send()
    for r in range(1, group):
        v2_copy(r).wait_send()
    for r in range(1, far):
        v3_copy(r).wait_send()
    for copy in (mixed_copy, tgrad_copy, vec_end, early_copy, late_copy):
        copy.wait()


def finish_kernel(
    mixed_in, tgrad_in, sums_in, vec_in, mixed_out, tgrad_out, qkv_out, wo_out, w1_out, w2_out, bias_out, gain_out,
    M, T, R, V, Q, O, A, B, bias, gain, sem,
):
    width = M.shape[1]
    pairs = HEADS // 2
    steps = 4
    rows = M.shape[0] // steps
    ins, outs = [], []

    def start(src, dst):
        copy = pltpu.make_async_copy(src, dst, sem.at[len(ins) + len(outs)])
        copy.start()
        return copy

    ins.append(start(sums_in, R))
    ins.append(start(vec_in, V))
    for i in range(steps):
        part = pl.ds(i * rows, rows)
        ins.append(start(tgrad_in.at[part], T.at[part]))
        ins.append(start(mixed_in.at[part], M.at[part]))
    ins[0].wait()
    for p in range(pairs):
        for t in range(2):
            c = 4 * width + 256 * p + 128 * t
            Q[:, t * width + p * 128 : t * width + p * 128 + 128] = R[:, c : c + 128].astype(F32)
    Q[:, 2 * width :] = R[:, 3 * width : 4 * width].astype(F32)
    outs.append(start(Q, qkv_out))
    for i, (ref, to) in enumerate(((O, wo_out), (A, w1_out), (B, w2_out))):
        ref[...] = R[:, i * width : i * width + width].astype(F32)
        outs.append(start(ref, to))
    ins[1].wait()
    bias[...] = V[0:7, :]
    gain[...] = V[8:10, :]
    outs.append(start(bias, bias_out))
    outs.append(start(gain, gain_out))
    for i in range(steps):
        part = pl.ds(i * rows, rows)
        ins[2 + 2 * i].wait()
        outs.append(start(T.at[part], tgrad_out.at[part]))
        ins[3 + 2 * i].wait()
        outs.append(start(M.at[part], mixed_out.at[part]))
    for copy in outs:
        copy.wait()


def call_layer(cells, fsdp, rows_n, width, lengths, generate, *args):
    vm = pl.BlockSpec(memory_space=pltpu.VMEM)
    sm = pl.BlockSpec(memory_space=pltpu.SMEM)
    hb = pl.BlockSpec(memory_space=pl.ANY)
    hbm = pl.BlockSpec(memory_space=pltpu.HBM)
    shard_rows = width // fsdp
    group = min(GROUP, cells)
    far = cells // group
    near = min(2, group)
    stride = group // near
    band, piece = 128 // near, 128 // group
    factor = 1.0 / (cells * fsdp)
    dma = pltpu.SemaphoreType.DMA
    outs = (((rows_n, width), BF), ((rows_n, width), F32), ((128, 6 * width), BF), ((16, 128), F32))
    far_n = max(far - 1, 1)
    LB = 256
    scratch = [
        ((rows_n, width), BF), ((rows_n, width), BF), ((1, rows_n), jnp.int32),
        ((width, 6 * width), BF), ((fsdp, 16, 128), F32), ((width, rows_n), BF), ((rows_n, 128), F32),
        ((4, rows_n, 128), BF), ((8, 128, rows_n), BF), ((4, rows_n, 128), BF), ((4, 128, rows_n), BF),
        ((4, rows_n, 128), BF), ((8, 80, rows_n), BF), ((8, rows_n, rows_n), BF),
        ((rows_n, width), BF), ((8, 64, rows_n), F32), ((8, 8, rows_n), F32), ((rows_n, 5 * width), BF),
        ((4, rows_n, 128), BF), ((8, 8, rows_n), F32), ((rows_n, rows_n), BF), ((rows_n, rows_n), BF),
        ((2, 128, rows_n), BF),
        ((rows_n, 4 * LB), F32), ((4, 8, LB), F32), ((rows_n, LB), BF), ((rows_n, LB), BF),
        ((16, width), F32),
        ((fsdp, 128, 6 * width), BF), ((2, 128, 6 * width), BF), ((2 * near - 1, band, 6 * width), BF),
        (((stride - 1) * piece, 6 * width), BF), ((far_n, 2 * piece, 2 * width), BF), ((128, 6 * width), BF),
        ((2 * piece, 6 * width), BF), ((2, 2 * group - 1, piece, 256), BF),
        ((fsdp, 16, 128), F32), ((fsdp - 1, 16, 128), F32), ((16, 128), F32), ((group - 1, 16, 128), F32),
        ((16, 128), F32), ((far_n, 16, 128), F32),
    ]
    sems = [
        (18,), (5,), (5, 3), (5, 3), (3,), (3,), (8, 2), (8, 2), (8, 2 * near - 1), (8, 2 * near - 1), (8,), (8,),
        (8, far_n), (8, far_n), (8,), (8,), (8,), (8,), (2,), (2,), (3,), (3,), (group - 1,), (group - 1,), (far_n,), (far_n,),
    ]
    results = pl.pallas_call(
        functools.partial(layer_kernel, cells, fsdp, factor),
        out_shape=[jax.ShapeDtypeStruct(s, t) for s, t in outs],
        in_specs=[sm] + [hb] * 7 + [vm] * 2,
        out_specs=[hb] * 4,
        scratch_shapes=[pltpu.VMEM(s, t) for s, t in scratch] + [dma(s) for s in sems],
        compiler_params=pltpu.CompilerParams(
            vmem_limit_bytes=63 * 2**20 + 2**19, collective_id=0, has_side_effects=True
        ),
        name="layer",
    )(lengths, generate, *args)
    finals = (
        ((rows_n, width), BF), ((rows_n, width), F32), ((shard_rows, 3 * width), F32), ((shard_rows, width), F32),
        ((shard_rows, width), F32), ((shard_rows, width), F32), ((7, width // fsdp), F32), ((2, width // fsdp), F32),
    )
    buffers = list(outs) + list(finals[2:])
    return pl.pallas_call(
        finish_kernel,
        out_shape=[jax.ShapeDtypeStruct(s, t) for s, t in finals],
        in_specs=[hbm] * 4,
        out_specs=[hbm] * 8,
        scratch_shapes=[pltpu.VMEM(s, t) for s, t in buffers] + [dma((24,))],
        compiler_params=pltpu.CompilerParams(vmem_limit_bytes=63 * 2**20),
        name="finish",
    )(*results)


def body(cells, fsdp, tokens, cotangent, lengths, generate, *weights):
    _, rows_n, width = tokens.shape
    mixed, tokens_grad, *grads = call_layer(
        cells, fsdp, rows_n, width, lengths, generate, tokens[0], cotangent[0], *weights
    )
    return (mixed[None], tokens_grad[None], *grads)


def solution(mesh):
    split = P(("cells", "fsdp"), None, None)
    rows, cols = P("fsdp", None), P(None, "fsdp")
    return jax.shard_map(
        functools.partial(body, mesh.shape["cells"], mesh.shape["fsdp"]),
        mesh=mesh,
        in_specs=(split, split, P(("cells", "fsdp")), P(("cells", "fsdp"), None), rows, rows, rows, rows, cols, cols),
        out_specs=(split, split, rows, rows, rows, rows, cols, cols),
        check_vma=False,
    )
```
